32 devices in a mesh: dp: 16 (over z, y, x), tensor: 2 (over core).
Axes of the slice: x: 2, y: 2, z: 4, core: 2. Of those that a mesh axis runs over, the one named last changes fastest.
Arguments:
- layer_input: bfloat16 [8192, 2048], P(('dp', 'tensor')), may hold values from -6 to 6
- upstream: bfloat16 [8192, 2048], P(('dp', 'tensor')), may hold values from -6 to 6
- doc_lengths: int32 [16, 6], P('dp'), may hold values from 1 to 448, 512 in all within a row
- token_valid: int32 [16, 512], P('dp'), may hold values 0 or 1
- query_weight: float32 [2048, 2048], P('dp', 'tensor'), may hold values from -0.125 to 0.125
- query_moment: float32 [2048, 2048], P('dp', 'tensor'), may hold values from -224 to 224
- query_second: float32 [2048, 2048], P('dp', 'tensor'), may hold values from 1310.72 to 5242.88
- query_shadow: float32 [2048, 2048], P('dp', 'tensor'), may hold values from -0.125 to 0.125
- keyval_weight: float32 [2048, 2, 256], P('dp', None, 'tensor'), may hold values from -0.125 to 0.125
- keyval_moment: float32 [2048, 2, 256], P('dp', None, 'tensor'), may hold values from -512 to 512
- keyval_second: float32 [2048, 2, 256], P('dp', None, 'tensor'), may hold values from 8192 to 32768
- keyval_shadow: float32 [2048, 2, 256], P('dp', None, 'tensor'), may hold values from -0.125 to 0.125
- mixing_weight: float32 [2048, 2048], P(('tensor', 'dp')), may hold values from -0.5 to 0.5
- mixing_moment: float32 [2048, 2048], P(('tensor', 'dp')), may hold values from -160 to 160
- mixing_second: float32 [2048, 2048], P(('tensor', 'dp')), may hold values from 737.28 to 2949.12
- mixing_shadow: float32 [2048, 2048], P(('tensor', 'dp')), may hold values from -0.5 to 0.5
- expand_weight: float32 [2048, 2, 5632], P('dp', None, 'tensor'), may hold values from -0.125 to 0.125
- expand_moment: float32 [2048, 2, 5632], P('dp', None, 'tensor'), may hold values from -224 to 224
- expand_second: float32 [2048, 2, 5632], P('dp', None, 'tensor'), may hold values from 1310.72 to 5242.88
- expand_shadow: float32 [2048, 2, 5632], P('dp', None, 'tensor'), may hold values from -0.125 to 0.125
- contract_weight: float32 [5632, 2048], P(('tensor', 'dp')), may hold values from -0.078125 to 0.078125
- contract_moment: float32 [5632, 2048], P(('tensor', 'dp')), may hold values from -256 to 256
- contract_second: float32 [5632, 2048], P(('tensor', 'dp')), may hold values from 2048 to 8192
- contract_shadow: float32 [5632, 2048], P(('tensor', 'dp')), may hold values from -0.078125 to 0.078125
- norms_weight: float32 [2, 2048], P(None, ('dp', 'tensor')), may hold values from 0.5 to 1.5
- norms_moment: float32 [2, 2048], P(None, ('dp', 'tensor')), may hold values from -256 to 256
- norms_second: float32 [2, 2048], P(None, ('dp', 'tensor')), may hold values from 2048 to 8192
- norms_shadow: float32 [2, 2048], P(None, ('dp', 'tensor')), may hold values from 0.5 to 1.5
Outputs:
- layer_output: bfloat16 [8192, 2048], P(('dp', 'tensor'))
- input_grad: float32 [8192, 2048], P(('dp', 'tensor'))
- query_master: float32 [2048, 2048], P('dp', 'tensor')
- query_momentum: float32 [2048, 2048], P('dp', 'tensor')
- query_variance: float32 [2048, 2048], P('dp', 'tensor')
- query_average: float32 [2048, 2048], P('dp', 'tensor')
- keyval_master: float32 [2048, 2, 256], P('dp', None, 'tensor')
- keyval_momentum: float32 [2048, 2, 256], P('dp', None, 'tensor')
- keyval_variance: float32 [2048, 2, 256], P('dp', None, 'tensor')
- keyval_average: float32 [2048, 2, 256], P('dp', None, 'tensor')
- mixing_master: float32 [2048, 2048], P(('tensor', 'dp'))
- mixing_momentum: float32 [2048, 2048], P(('tensor', 'dp'))
- mixing_variance: float32 [2048, 2048], P(('tensor', 'dp'))
- mixing_average: float32 [2048, 2048], P(('tensor', 'dp'))
- expand_master: float32 [2048, 2, 5632], P('dp', None, 'tensor')
- expand_momentum: float32 [2048, 2, 5632], P('dp', None, 'tensor')
- expand_variance: float32 [2048, 2, 5632], P('dp', None, 'tensor')
- expand_average: float32 [2048, 2, 5632], P('dp', None, 'tensor')
- contract_master: float32 [5632, 2048], P(('tensor', 'dp'))
- contract_momentum: float32 [5632, 2048], P(('tensor', 'dp'))
- contract_variance: float32 [5632, 2048], P(('tensor', 'dp'))
- contract_average: float32 [5632, 2048], P(('tensor', 'dp'))
- norms_master: float32 [2, 2048], P(None, ('dp', 'tensor'))
- norms_momentum: float32 [2, 2048], P(None, ('dp', 'tensor'))
- norms_variance: float32 [2, 2048], P(None, ('dp', 'tensor'))
- norms_average: float32 [2, 2048], P(None, ('dp', 'tensor'))
The draws below stay inside these ranges and needn't reach their ends.
Inputs may be any that keep to these rules, and one draw needn't show every extreme that they name: `doc_lengths`: each row sums to 512; its longest document has exactly 448 tokens.
All inputs are finite; a program needn't handle non-finite values. No bound on the sum of `token_valid` on one device may be relied on, other than what follows from the above.
Results may differ from the reference program's by a relative error of at most 0.015.
Values may be sent and summed in bfloat16 or wider, within the bound.
No kernel may reach another device: no remote copies, remote signals or barrier semaphores. Data moves between devices by JAX's collectives and lax.ppermute only.
A program may use at most 320 MiB of HBM per device.

```python
import math
from functools import partial
import jax
import jax.numpy as jnp
import numpy as np
from jax import lax

D = 2048
HEADS = 32
KV_HEADS = 4
HEAD_DIM = 64
FF = 5632
DOCS = 6
STEP = 5
GROUP = 512
TOKENS = 8192
N_DP = 16


def with_ends(values, own_key, smallest, top_value):
    dims = values.shape
    index_at = [jax.random.randint(jax.random.fold_in(own_key, axis), (), 0, dims[axis]) for axis in range(len(dims))]
    values = values.at[tuple(index_at)].set(smallest)
    longest = dims.index(max(dims))
    index_at[longest] = (index_at[longest] + 1) % dims[longest]
    return values.at[tuple(index_at)].set(top_value)


def levels(stream_key, extent, cuts, smallest, high):
    def one(axis_at, shards_of):
        heights = jax.random.uniform(jax.random.fold_in(jax.random.fold_in(stream_key, 6), axis_at), (shards_of,), jnp.float32, smallest / len(cuts), high / len(cuts))
        return jnp.repeat(jnp.exp(heights), extent[axis_at] // shards_of).reshape((-1,) + (1,) * (len(extent) - axis_at - 1))

    loudness = one(*cuts[0])
    for cut in cuts[1:]:
        loudness = loudness * one(*cut)
    return loudness


def profile(number_of, total, most, lean):
    portions = [(1 << 20) // math.isqrt(standing ** lean) + 1 for standing in range(2, number_of + 1)]
    spare, given = total - most - (number_of - 1), [1] * (number_of - 1)
    while spare > 0:
        candidates = [i for i in range(number_of - 1) if given[i] < most]
        mass, remaining = sum([portions[i] for i in candidates]), spare
        for i in candidates:
            more = min(most - given[i], max(1, remaining * portions[i] // mass), spare)
            given[i] = given[i] + more
            spare = spare - more
    return np.array([most] + given)


def uneven_parts(stream_key, amount, total, reach, skew):
    if amount == 2:
        one = jax.random.randint(stream_key, (), max(1, total - reach), min(reach, total - 1) + 1)
        return jnp.stack([one, total - one])
    tallies = jnp.asarray(profile(amount, total, reach, skew), jnp.int32)
    couples = (amount - 1) // 2
    donor, sink = tallies[1:1 + 2 * couples:2], tallies[2:2 + 2 * couples:2]
    room = jnp.minimum(donor - 1, reach - sink)
    passed = jax.random.randint(jax.random.fold_in(stream_key, 1), (couples,), 0, 1 << 20) % (room + 1)
    tallies = tallies.at[1:1 + 2 * couples:2].set(donor - passed).at[2:2 + 2 * couples:2].set(sink + passed)
    return tallies[jax.random.permutation(jax.random.fold_in(stream_key, 2), amount)]


def scatter_about(rng, dims, deviation, limit, shards=(), kind=jnp.bfloat16):
    values = jax.random.normal(rng, dims, jnp.float32) * deviation
    if len(shards) > 0:
        values = levels(rng, dims, shards, -0.22, 0.18) * values
    return jnp.clip(values, min=-limit, max=limit).astype(kind)


def setup_inputs(seed: int = 0) -> dict:
    key_of = jax.random.split(jax.random.key(seed), 29)
    layer_input = scatter_about(key_of[0], (TOKENS, D), 1.0, 6.0, ((0, 32),))
    upstream = scatter_about(key_of[1], (TOKENS, D), 1.0, 6.0, ((0, 32),))
    doc_lengths = jax.vmap(lambda own: uneven_parts(own, DOCS, GROUP, GROUP - GROUP // 8, 2))(jax.random.split(key_of[2], N_DP)).reshape((N_DP, DOCS)).astype(jnp.int32)
    token_valid = with_ends((jax.random.randint(key_of[3], (N_DP, GROUP), 0, 8) < 7).astype(jnp.int32), jax.random.fold_in(key_of[3], 1), 0, 1)
    query_weight = scatter_about(key_of[4], (D, HEADS * HEAD_DIM), D ** -0.5, 0.125, ((0, 16), (1, 2)), jnp.float32)
    query_moment = scatter_about(key_of[5], (D, HEADS * HEAD_DIM), (0.4 * TOKENS ** 0.5), 224.0, ((0, 16), (1, 2)), jnp.float32)
    query_second = jnp.clip(jnp.exp(math.log(5242.88) - 1.3862944 * jax.random.uniform(key_of[6], (D, HEADS * HEAD_DIM), jnp.float32) ** levels(key_of[6], (D, HEADS * HEAD_DIM), ((0, 16), (1, 2)), -0.2, 0.2)), 1310.72, 5242.88)
    query_shadow = scatter_about(key_of[7], (D, HEADS * HEAD_DIM), D ** -0.5, 0.125, ((0, 16), (1, 2)), jnp.float32)
    keyval_weight = scatter_about(key_of[8], (D, 2, KV_HEADS * HEAD_DIM), D ** -0.5, 0.125, ((0, 16), (2, 2)), jnp.float32)
    keyval_moment = scatter_about(key_of[9], (D, 2, KV_HEADS * HEAD_DIM), (1.0 * TOKENS ** 0.5), 512.0, ((0, 16), (2, 2)), jnp.float32)
    keyval_second = jnp.clip(jnp.exp(math.log(32768.0) - 1.3862944 * jax.random.uniform(key_of[10], (D, 2, KV_HEADS * HEAD_DIM), jnp.float32) ** levels(key_of[10], (D, 2, KV_HEADS * HEAD_DIM), ((0, 16), (2, 2)), -0.2, 0.2)), 8192.0, 32768.0)
    keyval_shadow = scatter_about(key_of[11], (D, 2, KV_HEADS * HEAD_DIM), D ** -0.5, 0.125, ((0, 16), (2, 2)), jnp.float32)
    mixing_weight = scatter_about(key_of[12], (HEADS * HEAD_DIM, D), (HEADS * HEAD_DIM // 16) ** -0.5, 0.5, ((0, 32),), jnp.float32)
    mixing_moment = scatter_about(key_of[13], (HEADS * HEAD_DIM, D), (0.3 * TOKENS ** 0.5), 160.0, ((0, 32),), jnp.float32)
    mixing_second = jnp.clip(jnp.exp(math.log(2949.12) - 1.3862944 * jax.random.uniform(key_of[14], (HEADS * HEAD_DIM, D), jnp.float32) ** levels(key_of[14], (HEADS * HEAD_DIM, D), ((0, 32),), -0.2, 0.2)), 737.28, 2949.12)
    mixing_shadow = scatter_about(key_of[15], (HEADS * HEAD_DIM, D), (HEADS * HEAD_DIM // 16) ** -0.5, 0.5, ((0, 32),), jnp.float32)
    expand_weight = scatter_about(key_of[16], (D, 2, FF), D ** -0.5, 0.125, ((0, 16), (2, 2)), jnp.float32)
    expand_moment = scatter_about(key_of[17], (D, 2, FF), (0.4 * TOKENS ** 0.5), 224.0, ((0, 16), (2, 2)), jnp.float32)
    expand_second = jnp.clip(jnp.exp(math.log(5242.88) - 1.3862944 * jax.random.uniform(key_of[18], (D, 2, FF), jnp.float32) ** levels(key_of[18], (D, 2, FF), ((0, 16), (2, 2)), -0.2, 0.2)), 1310.72, 5242.88)
    expand_shadow = scatter_about(key_of[19], (D, 2, FF), D ** -0.5, 0.125, ((0, 16), (2, 2)), jnp.float32)
    contract_weight = scatter_about(key_of[20], (FF, D), FF ** -0.5, 0.078125, ((0, 32),), jnp.float32)
    contract_moment = scatter_about(key_of[21], (FF, D), (0.5 * TOKENS ** 0.5), 256.0, ((0, 32),), jnp.float32)
    contract_second = jnp.clip(jnp.exp(math.log(8192.0) - 1.3862944 * jax.random.uniform(key_of[22], (FF, D), jnp.float32) ** levels(key_of[22], (FF, D), ((0, 32),), -0.2, 0.2)), 2048.0, 8192.0)
    contract_shadow = scatter_about(key_of[23], (FF, D), FF ** -0.5, 0.078125, ((0, 32),), jnp.float32)
    norms_weight = jnp.clip(1.0 + 0.1 * jax.random.normal(key_of[24], (2, D), jnp.float32), 0.5, 1.5)
    norms_moment = scatter_about(key_of[25], (2, D), (0.5 * TOKENS ** 0.5), 256.0, ((1, 32),), jnp.float32)
    norms_second = jnp.clip(jnp.exp(math.log(8192.0) - 1.3862944 * jax.random.uniform(key_of[26], (2, D), jnp.float32) ** levels(key_of[26], (2, D), ((1, 32),), -0.2, 0.2)), 2048.0, 8192.0)
    norms_shadow = jnp.clip(1.0 + 0.1 * jax.random.normal(key_of[27], (2, D), jnp.float32), 0.5, 1.5)
    return dict(layer_input=layer_input, upstream=upstream, doc_lengths=doc_lengths, token_valid=token_valid, query_weight=query_weight, query_moment=query_moment, query_second=query_second, query_shadow=query_shadow, keyval_weight=keyval_weight, keyval_moment=keyval_moment, keyval_second=keyval_second, keyval_shadow=keyval_shadow, mixing_weight=mixing_weight, mixing_moment=mixing_moment, mixing_second=mixing_second, mixing_shadow=mixing_shadow, expand_weight=expand_weight, expand_moment=expand_moment, expand_second=expand_second, expand_shadow=expand_shadow, contract_weight=contract_weight, contract_moment=contract_moment, contract_second=contract_second, contract_shadow=contract_shadow, norms_weight=norms_weight, norms_moment=norms_moment, norms_second=norms_second, norms_shadow=norms_shadow)


@jax.custom_vjp
def low(v):
    return lax.optimization_barrier(v.astype(jnp.bfloat16)).astype(jnp.float32)

@jax.custom_vjp
def low_back(v):
    return v

def low_keep(v):
    return (low(v), None)

def low_pass(kept, grad):
    return (grad,)

def back_keep(v):
    return (v, None)

def back_low(kept, grad):
    return (low(grad),)
low.defvjp(low_keep, low_pass)
low_back.defvjp(back_keep, back_low)
NORM_EPS = 1e-05
NEG_FILL = -1e+30
ROPE_BASE = 10000.0
BETA_ONE = 0.5
BETA_TWO = 0.5
ADAM_EPS = 1e-08
WEIGHT_DECAY = 0.1
MATRIX_RATE = 0.02
GAIN_RATE = 0.2
EMA_KEEP = 0.9
GAIN_KEEP = 0.5
HIGH = lax.Precision.HIGHEST

def normalize(field_rows, gain_row):
    factor = lax.rsqrt(lax.optimization_barrier(jnp.mean(field_rows * field_rows, axis=-1, keepdims=True)) + NORM_EPS)
    return field_rows * factor * gain_row

def rotate(field, cosine_table, sine_table):
    half_dim = field.shape[-1] // 2
    first_half = field[..., :half_dim]
    second_half = field[..., half_dim:]
    return jnp.concatenate([first_half * cosine_table - second_half * sine_table, second_half * cosine_table + first_half * sine_table], axis=-1)

def layout(lengths, valid_keys):
    group_len = valid_keys.shape[0]
    places = jnp.arange(group_len, dtype=jnp.int32)
    doc_ends = jnp.cumsum(lengths).astype(jnp.int32)
    doc_starts = (doc_ends - lengths).astype(jnp.int32)
    segment = lax.optimization_barrier(jnp.sum((doc_ends[None, :] <= places[:, None]).astype(jnp.int32), axis=1))
    owned_doc = segment[:, None] == jnp.arange(lengths.shape[0], dtype=jnp.int32)[None, :]
    position = places - lax.optimization_barrier(jnp.sum(jnp.where(owned_doc, doc_starts[None, :], 0), axis=1)).astype(jnp.int32)
    allowed = (segment[:, None] == segment[None, :]) & (places[None, :] <= places[:, None]) & ((valid_keys[None, :] == 1) | (places[:, None] == places[None, :]))
    return (position, allowed)

def rope_tables(position, head_size):
    half_dim = head_size // 2
    inverse = ROPE_BASE ** (-(2.0 * jnp.arange(half_dim, dtype=jnp.float32)) / head_size)
    angles = position.astype(jnp.float32)[:, None] * inverse[None, :]
    return (jnp.cos(angles)[:, None, :], jnp.sin(angles)[:, None, :])

def group_layer(weights, group_item):
    query_low, keyval_low, mixing_low, expand_low, contract_low, gain_rows = weights
    input_rows, lengths, valid_keys = group_item
    position, allowed = layout(lengths, valid_keys)
    cosine_table, sine_table = rope_tables(position, HEAD_DIM)
    group_len = input_rows.shape[0]
    normed = low(normalize(input_rows, gain_rows[0]))
    query_pre = low_back(jnp.dot(normed, query_low, precision=HIGH)).reshape(group_len, HEADS, HEAD_DIM)
    keyval_pre = low_back(jnp.einsum('gd,dsc->gsc', normed, keyval_low, precision=HIGH))
    queries = low(rotate(query_pre, cosine_table, sine_table))
    keys = low(rotate(keyval_pre[:, 0].reshape(group_len, KV_HEADS, HEAD_DIM), cosine_table, sine_table))
    values = low(keyval_pre[:, 1].reshape(group_len, KV_HEADS, HEAD_DIM))
    group_ratio = HEADS // KV_HEADS
    grouped = queries.reshape(group_len, KV_HEADS, group_ratio, HEAD_DIM)
    scores = low_back(jnp.einsum('gjre,kje->jrgk', grouped, keys, precision=HIGH) * HEAD_DIM ** (-0.5))
    masked = jnp.where(allowed[None, None], scores, NEG_FILL)
    largest = lax.optimization_barrier(jnp.max(masked, axis=-1, keepdims=True))
    exp_scores = jnp.exp(masked - largest)
    soft_probs = low(exp_scores / lax.optimization_barrier(jnp.sum(exp_scores, axis=-1, keepdims=True)))
    mixed = low(low_back(jnp.einsum('jrgk,kje->gjre', soft_probs, values, precision=HIGH))).reshape(group_len, HEADS * HEAD_DIM)
    attended = low_back(jnp.dot(mixed, mixing_low, precision=HIGH))
    middle = input_rows + attended
    normed_two = low(normalize(middle, gain_rows[1]))
    gate_up = low_back(jnp.einsum('gd,dsf->gsf', normed_two, expand_low, precision=HIGH))
    hidden = low(jax.nn.silu(gate_up[:, 0]) * gate_up[:, 1])
    return low(middle + low_back(jnp.dot(hidden, contract_low, precision=HIGH)))

def forward(input_rows, query_full, keyval_full, mixing_full, expand_full, contract_full, gain_rows, lengths, valid_keys):
    lowered = (low(query_full), low(keyval_full), low(mixing_full), low(expand_full), low(contract_full), gain_rows)
    blocked = input_rows.reshape(N_DP, GROUP, D)
    group_step = jax.checkpoint(group_layer)
    outputs = lax.map(lambda group_item: group_step(lowered, group_item), (blocked, lengths, valid_keys))
    return outputs.reshape(N_DP * GROUP, D)

def adamw(grad_value, weight, moment, second, shadow, step_rate, decay_rate, keep_rate):
    moment_new = BETA_ONE * moment + (1.0 - BETA_ONE) * grad_value
    second_new = BETA_TWO * second + (1.0 - BETA_TWO) * grad_value * grad_value
    moment_hat = moment_new / (1.0 - BETA_ONE ** STEP)
    second_hat = second_new / (1.0 - BETA_TWO ** STEP)
    weight_new = weight - step_rate * (moment_hat / (jnp.sqrt(second_hat) + ADAM_EPS) + decay_rate * weight)
    shadow_new = keep_rate * shadow + (1.0 - keep_rate) * weight_new
    return (weight_new, moment_new, second_new, shadow_new)

def reference(layer_input, upstream, doc_lengths, token_valid, query_weight, query_moment, query_second, query_shadow, keyval_weight, keyval_moment, keyval_second, keyval_shadow, mixing_weight, mixing_moment, mixing_second, mixing_shadow, expand_weight, expand_moment, expand_second, expand_shadow, contract_weight, contract_moment, contract_second, contract_shadow, norms_weight, norms_moment, norms_second, norms_shadow):
    bound = partial(forward, lengths=doc_lengths, valid_keys=token_valid)
    result, pull = jax.vjp(bound, layer_input.astype(jnp.float32), query_weight, keyval_weight, mixing_weight, expand_weight, contract_weight, norms_weight)
    gradients = pull(upstream.astype(jnp.float32))
    input_grad = gradients[0]
    query_master, query_momentum, query_variance, query_average = adamw(gradients[1], query_weight, query_moment, query_second, query_shadow, MATRIX_RATE, WEIGHT_DECAY, EMA_KEEP)
    keyval_master, keyval_momentum, keyval_variance, keyval_average = adamw(gradients[2], keyval_weight, keyval_moment, keyval_second, keyval_shadow, MATRIX_RATE, WEIGHT_DECAY, EMA_KEEP)
    mixing_master, mixing_momentum, mixing_variance, mixing_average = adamw(gradients[3], mixing_weight, mixing_moment, mixing_second, mixing_shadow, MATRIX_RATE, WEIGHT_DECAY, EMA_KEEP)
    expand_master, expand_momentum, expand_variance, expand_average = adamw(gradients[4], expand_weight, expand_moment, expand_second, expand_shadow, MATRIX_RATE, WEIGHT_DECAY, EMA_KEEP)
    contract_master, contract_momentum, contract_variance, contract_average = adamw(gradients[5], contract_weight, contract_moment, contract_second, contract_shadow, MATRIX_RATE, WEIGHT_DECAY, EMA_KEEP)
    norms_master, norms_momentum, norms_variance, norms_average = adamw(gradients[6], norms_weight, norms_moment, norms_second, norms_shadow, GAIN_RATE, 0.0, GAIN_KEEP)
    return (result.astype(jnp.bfloat16), input_grad, query_master, query_momentum, query_variance, query_average, keyval_master, keyval_momentum, keyval_variance, keyval_average, mixing_master, mixing_momentum, mixing_variance, mixing_average, expand_master, expand_momentum, expand_variance, expand_average, contract_master, contract_momentum, contract_variance, contract_average, norms_master, norms_momentum, norms_variance, norms_average)
```

```python
import jax
import jax.numpy as jnp
from jax import lax
from jax.experimental import pallas as pl
from jax.experimental.pallas import tpu as pltpu
from jax.sharding import PartitionSpec as P

HEAD_DIM = 64
STEP = 5


NORM_EPS = 1e-05
NEG_FILL = -1e30
ROPE_BASE = 10000.0
BETA_ONE = 0.5
BETA_TWO = 0.5
ADAM_EPS = 1e-08
WEIGHT_DECAY = 0.1
MATRIX_RATE = 0.02
GAIN_RATE = 0.2
EMA_KEEP = 0.9
GAIN_KEEP = 0.5
CONTRACT_LAST = (((1,), (1,)), ((), ()))
CONTRACT_FIRST = (((0,), (0,)), ((), ()))


def normalize(field_rows, gain_row):
    factor = lax.rsqrt(jnp.mean(field_rows * field_rows, axis=-1, keepdims=True) + NORM_EPS)
    return field_rows * factor * gain_row


def rotate(field, cosine_table, sine_table):
    half_dim = field.shape[-1] // 2
    first_half = field[..., :half_dim]
    second_half = field[..., half_dim:]
    return jnp.concatenate(
        [
            first_half * cosine_table - second_half * sine_table,
            second_half * cosine_table + first_half * sine_table,
        ],
        axis=-1,
    )


def layout(lengths, valid_keys, places):
    doc_ends = jnp.cumsum(lengths)
    doc_starts = doc_ends - lengths
    segment = jnp.sum((doc_ends[None, :] <= places[:, None]).astype(jnp.int32), axis=1)
    owned_doc = segment[:, None] == jnp.arange(lengths.shape[0], dtype=jnp.int32)[None, :]
    position = places - jnp.sum(jnp.where(owned_doc, doc_starts[None, :], 0), axis=1)
    allowed = (
        (segment[:, None] == segment[None, :])
        & (places[None, :] <= places[:, None])
        & ((valid_keys[None, :] == 1) | (places[:, None] == places[None, :]))
    )
    return (position, allowed)


def rope_tables(position, head_size):
    half_dim = head_size // 2
    inverse = ROPE_BASE ** (-(2.0 * jnp.arange(half_dim, dtype=jnp.float32)) / head_size)
    angles = position.astype(jnp.float32)[:, None] * inverse[None, :]
    return (jnp.cos(angles)[:, None, :], jnp.sin(angles)[:, None, :])


def adamw(grad_value, weight, moment, second, shadow, step_rate, decay_rate, keep_rate):
    moment_new = BETA_ONE * moment + (1.0 - BETA_ONE) * grad_value
    second_new = BETA_TWO * second + (1.0 - BETA_TWO) * grad_value * grad_value
    moment_hat = moment_new / (1.0 - BETA_ONE**STEP)
    second_hat = second_new / (1.0 - BETA_TWO**STEP)
    weight_new = weight - step_rate * (
        moment_hat / (jnp.sqrt(second_hat) + ADAM_EPS) + decay_rate * weight
    )
    shadow_new = keep_rate * shadow + (1.0 - keep_rate) * weight_new
    return (weight_new, moment_new, second_new, shadow_new)


def cast_halves(weight, pair_bit):
    row_count, planes, columns = weight.shape
    half = columns // 2

    def kernel(bit_ref, weight_ref, keep_ref, send_ref):
        for plane in range(planes):
            low = weight_ref[:, plane, :half].astype(jnp.bfloat16)
            high = weight_ref[:, plane, half:].astype(jnp.bfloat16)
            at = pl.ds(plane * half, half)

            @pl.when(bit_ref[0] == 0)
            def _():
                keep_ref[:, at] = low
                send_ref[:, at] = high

            @pl.when(bit_ref[0] != 0)
            def _():
                keep_ref[:, at] = high
                send_ref[:, at] = low

    out = jax.ShapeDtypeStruct((row_count, planes * half), jnp.bfloat16)
    step = 16
    return pl.pallas_call(
        kernel,
        grid_spec=pltpu.PrefetchScalarGridSpec(
            num_scalar_prefetch=1,
            grid=(row_count // step,),
            in_specs=[pl.BlockSpec((step, planes, columns), lambda i, bit: (i, 0, 0))],
            out_specs=[pl.BlockSpec((step, planes * half), lambda i, bit: (i, 0))] * 2,
        ),
        out_shape=(out, out),
        compiler_params=pltpu.CompilerParams(vmem_limit_bytes=32 * 2**20),
    )(pair_bit.reshape(1), weight)


def cast_projections(query, keyval, pair_bit):
    row_count, columns = query.shape
    half, width = columns // 2, keyval.shape[2]

    def kernel(bit_ref, query_ref, keyval_ref, keep_ref, send_ref):
        left = lax.broadcasted_iota(jnp.int32, (row_count, width), 1) < width // 2
        key, value = keyval_ref[:, 0, :], keyval_ref[:, 1, :]
        low = jnp.where(left, key, pltpu.roll(value, width // 2, 1)).astype(jnp.bfloat16)
        high = jnp.where(left, pltpu.roll(key, width // 2, 1), value).astype(jnp.bfloat16)

        def store(low_ref, high_ref):
            low_ref[:, :half] = query_ref[:, :half].astype(jnp.bfloat16)
            high_ref[:, :half] = query_ref[:, half:].astype(jnp.bfloat16)
            low_ref[:, half:] = low
            high_ref[:, half:] = high

        @pl.when(bit_ref[0] == 0)
        def _():
            store(keep_ref, send_ref)

        @pl.when(bit_ref[0] != 0)
        def _():
            store(send_ref, keep_ref)

    out = jax.ShapeDtypeStruct((row_count, half + width), jnp.bfloat16)
    return pl.pallas_call(
        kernel,
        in_specs=[pl.BlockSpec(memory_space=pltpu.SMEM)]
        + [pl.BlockSpec(memory_space=pltpu.VMEM)] * 2,
        out_specs=[pl.BlockSpec(memory_space=pltpu.VMEM)] * 2,
        out_shape=(out, out),
        compiler_params=pltpu.CompilerParams(vmem_limit_bytes=16 * 2**20),
    )(pair_bit.reshape(1), query, keyval)


def projection_update(parts, pair_bit, queries, keyvals):
    row_count, columns = queries[0].shape
    half, width = columns // 2, keyvals[0].shape[2]

    def kernel(bit_ref, *refs):
        parts, olds, news = refs[:4], refs[4:12], refs[12:]
        one, two, three, four = [ref[...].astype(jnp.float32) for ref in parts]
        own, other = one + two, three + four
        mine = bit_ref[0] == 0
        low, high = jnp.where(mine, own, other), jnp.where(mine, other, own)
        left = lax.broadcasted_iota(jnp.int32, (row_count, width), 1) < width // 2
        low_pair, high_pair = low[:, half:], high[:, half:]
        grads = (
            (0, (slice(None), slice(0, half)), low[:, :half]),
            (0, (slice(None), slice(half, columns)), high[:, :half]),
            (4, (slice(None), 0), jnp.where(left, low_pair, pltpu.roll(high_pair, width // 2, 1))),
            (4, (slice(None), 1), jnp.where(left, pltpu.roll(low_pair, width // 2, 1), high_pair)),
        )
        for first, where, grad in grads:
            results = adamw(
                grad,
                *[ref[where] for ref in olds[first : first + 4]],
                MATRIX_RATE,
                WEIGHT_DECAY,
                EMA_KEEP,
            )
            for ref, result in zip(news[first : first + 4], results):
                ref[where] = result

    outs = [jax.ShapeDtypeStruct(old.shape, jnp.float32) for old in queries + keyvals]
    results = pl.pallas_call(
        kernel,
        in_specs=[pl.BlockSpec(memory_space=pltpu.SMEM)]
        + [pl.BlockSpec(memory_space=pltpu.VMEM)] * 12,
        out_specs=[pl.BlockSpec(memory_space=pltpu.VMEM)] * 8,
        out_shape=outs,
        compiler_params=pltpu.CompilerParams(vmem_limit_bytes=32 * 2**20),
    )(pair_bit.reshape(1), *parts, *queries, *keyvals)
    return results[:4], results[4:]


def expand_update(parts, pair_bit, weight, moment, second, shadow):
    row_count, planes, columns = weight.shape
    half = columns // 2
    step = 16

    def kernel(bit_ref, *refs):
        parts, olds, news = refs[:8], refs[8:12], refs[12:]
        for plane in range(planes):
            one, two, three, four = [
                ref[...].astype(jnp.float32) for ref in parts[plane * 4 : plane * 4 + 4]
            ]
            own, other = one + two, three + four
            mine = bit_ref[0] == 0
            for side, grad in (
                (0, jnp.where(mine, own, other)),
                (1, jnp.where(mine, other, own)),
            ):
                where = (slice(None), plane, pl.ds(side * half, half))
                results = adamw(
                    grad, *[ref[where] for ref in olds], MATRIX_RATE, WEIGHT_DECAY, EMA_KEEP
                )
                for ref, result in zip(news, results):
                    ref[where] = result

    def state_spec():
        return pl.BlockSpec((step, planes, columns), lambda i, bit: (i, 0, 0))

    out = jax.ShapeDtypeStruct(weight.shape, jnp.float32)
    return pl.pallas_call(
        kernel,
        grid_spec=pltpu.PrefetchScalarGridSpec(
            num_scalar_prefetch=1,
            grid=(row_count // step,),
            in_specs=[pl.BlockSpec((step, half), lambda i, bit: (i, 0))] * 8
            + [state_spec() for _ in range(4)],
            out_specs=[state_spec() for _ in range(4)],
        ),
        out_shape=(out,) * 4,
        compiler_params=pltpu.CompilerParams(vmem_limit_bytes=48 * 2**20),
    )(pair_bit.reshape(1), *parts, weight, moment, second, shadow)


def per_device(
    layer_input,
    upstream,
    doc_lengths,
    token_valid,
    query_weight,
    query_moment,
    query_second,
    query_shadow,
    keyval_weight,
    keyval_moment,
    keyval_second,
    keyval_shadow,
    mixing_weight,
    mixing_moment,
    mixing_second,
    mixing_shadow,
    expand_weight,
    expand_moment,
    expand_second,
    expand_shadow,
    contract_weight,
    contract_moment,
    contract_second,
    contract_shadow,
    norms_weight,
    norms_moment,
    norms_second,
    norms_shadow,
):
    bf_type = jnp.bfloat16
    fl_type = jnp.float32
    dp_count = lax.axis_size("dp")
    low_count = dp_count // 4
    dp_index = lax.axis_index("dp")
    outer_bit = dp_index // (2 * low_count)
    pair_bit = (dp_index // low_count) % 2
    core_bit = lax.axis_index("tensor")
    low_groups = [[base * low_count + low for low in range(low_count)] for base in range(4)]

    def move(value, target):
        return lax.ppermute(
            value,
            "dp",
            [
                (place * low_count + low, goal * low_count + low)
                for place, goal in target.items()
                for low in range(low_count)
            ],
        )

    def swap(value, flip):
        return move(value, {place: place ^ flip for place in range(4)})

    def swap_pair(value):
        return swap(value, 1)

    def swap_core(value):
        return lax.ppermute(value, "tensor", [(0, 1), (1, 0)])

    def after(value, *earlier):
        return lax.optimization_barrier((value,) + earlier)[0]

    def pick(bit, zero, one):
        return jnp.where(bit == 0, zero, one)

    def gather_low(blocks):
        return lax.all_gather(blocks, "dp", axis=1, tiled=True, axis_index_groups=low_groups)

    def scatter_low(blocks):
        return lax.psum_scatter(
            blocks, "dp", scatter_dimension=1, tiled=True, axis_index_groups=low_groups
        )

    own_rows, model_width = query_weight.shape[0], norms_weight.shape[1] * dp_count * 2

    def exchange_columns(keep, send):
        return keep, swap(send, 1), swap(keep, 2), swap(send, 3)

    def gather_columns(keep, one, two, three):
        low_pair = [pick(pair_bit, keep, one), pick(pair_bit, one, keep)]
        high_pair = [pick(pair_bit, two, three), pick(pair_bit, three, two)]
        quad = pick(outer_bit, jnp.stack(low_pair + high_pair), jnp.stack(high_pair + low_pair))
        return gather_low(quad).reshape(model_width, keep.shape[-1])

    def exchange_owned(rows):
        return rows, move(rows, {0: 2, 1: 0, 2: 3, 3: 1}), move(rows, {1: 2, 2: 1})

    def gather_owned(rows, first, second):
        second = pick(outer_bit ^ pair_bit, rows, second)
        both = pick(outer_bit, jnp.stack([second, first]), jnp.stack([first, second]))
        return gather_low(both).reshape(2 * low_count * rows.shape[0], rows.shape[1])

    def gather_tokens(rows):
        away = swap_pair(rows)
        return jnp.concatenate([rows, swap_core(rows), away, swap_core(away)])

    def scatter_tokens(partial):
        own, across, away, far = jnp.split(partial, 4)

        def over_cores(mine, sent):
            return mine + swap_core(sent.astype(bf_type)).astype(fl_type)

        moved = swap_pair(over_cores(away, far).astype(bf_type))
        return over_cores(own, across) + moved.astype(fl_type)

    qkv_keep, qkv_send = cast_projections(query_weight, keyval_weight, pair_bit)
    other_lengths, other_valid = swap_pair(doc_lengths), swap_pair(token_valid)
    qkv_moved = exchange_columns(qkv_keep, qkv_send)
    gain_copies = jnp.broadcast_to(
        after(norms_weight, qkv_keep)[None], (2 * dp_count,) + norms_weight.shape
    )
    gain_rows = lax.all_to_all(
        gain_copies, ("dp", "tensor"), split_axis=0, concat_axis=0, tiled=True
    )
    gain_rows = gain_rows.transpose(1, 0, 2).reshape(2, model_width)
    input_rows = layer_input.astype(fl_type)
    normed = normalize(input_rows, gain_rows[0]).astype(bf_type)
    normed_all = gather_tokens(normed)
    mixing_moved = exchange_owned(after(mixing_weight, normed).astype(bf_type))
    expand_keep, expand_send = cast_halves(after(expand_weight, normed), pair_bit)
    expand_moved = exchange_columns(expand_keep, expand_send)
    contract_moved = exchange_owned(after(contract_weight, expand_send).astype(bf_type))
    qkv_low = gather_columns(*after(qkv_moved, normed))
    mixing_low = gather_owned(*mixing_moved)
    group_len = token_valid.shape[1]
    places = (
        jnp.arange(group_len, dtype=jnp.int32) + core_bit * (group_len // 2)
    ) % group_len

    def ordered_valid(valid):
        first, second = valid[: group_len // 2], valid[group_len // 2 :]
        return pick(
            core_bit, jnp.concatenate([first, second]), jnp.concatenate([second, first])
        )

    position_one, allowed_one = layout(doc_lengths[0], ordered_valid(token_valid[0]), places)
    position_two, allowed_two = layout(other_lengths[0], ordered_valid(other_valid[0]), places)
    allowed = (allowed_one, allowed_two)
    cosine_table, sine_table = rope_tables(
        jnp.concatenate([position_one, position_two]), HEAD_DIM
    )
    token_count = 2 * group_len
    query_width = query_weight.shape[1] // 2
    key_width = keyval_weight.shape[2] // 2
    head_count = query_width // HEAD_DIM
    kv_count = key_width // HEAD_DIM
    group_ratio = head_count // kv_count
    hidden_width = expand_weight.shape[2] // 2
    factor = HEAD_DIM ** (-0.5)
    qkv_pre = jnp.dot(normed_all, qkv_low, preferred_element_type=fl_type)
    queries = rotate(
        qkv_pre[:, :query_width].reshape(token_count, head_count, HEAD_DIM),
        cosine_table,
        sine_table,
    ).astype(bf_type)
    keys = rotate(
        qkv_pre[:, query_width : query_width + key_width].reshape(token_count, kv_count, HEAD_DIM),
        cosine_table,
        sine_table,
    ).astype(bf_type)
    values = (
        qkv_pre[:, query_width + key_width :]
        .reshape(token_count, kv_count, HEAD_DIM)
        .astype(bf_type)
    )

    expand_low = gather_columns(*after(expand_moved, queries))
    contract_low = gather_owned(*after(contract_moved, queries))

    def part(array, group_index, kv_index, heads):
        return array[
            group_index * group_len : (group_index + 1) * group_len,
            kv_index * heads : (kv_index + 1) * heads,
        ]

    def head_scores(group_index, kv_index):
        query_block = part(queries, group_index, kv_index, group_ratio)
        key_block = part(keys, group_index, kv_index, 1)[:, 0]
        raw_scores = (
            jnp.einsum("gre,ke->rgk", query_block, key_block, preferred_element_type=fl_type)
            * factor
        )
        return (query_block, key_block, jnp.where(allowed[group_index][None], raw_scores, NEG_FILL))

    mixed_groups = []
    log_totals = {}
    for group_index in range(2):
        mixed_parts = []
        for kv_index in range(kv_count):
            _, _, masked = head_scores(group_index, kv_index)
            largest = jnp.max(masked, axis=-1, keepdims=True)
            exp_scores = jnp.exp(masked - largest)
            totals = jnp.sum(exp_scores, axis=-1, keepdims=True)
            soft_probs = (exp_scores / totals).astype(bf_type)
            log_totals[group_index, kv_index] = largest + jnp.log(totals)
            mixed_parts.append(
                jnp.einsum(
                    "rgk,ke->gre",
                    soft_probs,
                    part(values, group_index, kv_index, 1)[:, 0],
                    preferred_element_type=fl_type,
                )
            )
        mixed_groups.append(jnp.concatenate(mixed_parts, axis=1))
    mixed = jnp.concatenate(mixed_groups).reshape(token_count, query_width).astype(bf_type)
    attended = scatter_tokens(jnp.dot(mixed, mixing_low, preferred_element_type=fl_type))
    middle = input_rows + attended
    normed_two = normalize(middle, gain_rows[1]).astype(bf_type)
    normed_two_all = gather_tokens(normed_two)
    gate_up = jnp.dot(normed_two_all, expand_low, preferred_element_type=fl_type)
    gate, up = gate_up[:, :hidden_width], gate_up[:, hidden_width:]
    gate_sig = jax.nn.sigmoid(gate)
    gate_act = gate * gate_sig
    hidden = (gate_act * up).astype(bf_type)
    out_grad = upstream.astype(fl_type)
    out_grad_all = gather_tokens(after(upstream, normed_two))

    def reduce_columns(full):
        return scatter_low(full.reshape(4, low_count * own_rows, full.shape[1]))

    def scatter_columns(reduced):
        place = 2 * outer_bit + pair_bit
        kept, one, two, three = [
            lax.dynamic_index_in_dim(reduced, place ^ flip, 0, keepdims=False) for flip in range(4)
        ]
        return kept, swap(two, 2), swap(one, 1), swap(three, 3)

    def reduce_owned(full):
        return scatter_low(full.reshape(2, full.shape[0] // 2, full.shape[1]))

    def scatter_owned(reduced):
        first = move(pick(outer_bit, reduced[1], reduced[0]), {0: 1, 1: 3, 2: 0, 3: 2})
        rest = pick(outer_bit, reduced[0], reduced[1])
        second = pick(outer_bit ^ pair_bit, rest, move(rest, {1: 2, 2: 1}))
        return first.astype(fl_type) + second.astype(fl_type)

    contract_full = lax.dot_general(
        hidden, out_grad_all, CONTRACT_FIRST, preferred_element_type=fl_type
    ).astype(bf_type)
    contract_reduced = reduce_owned(contract_full)
    hidden_grad = lax.dot_general(
        after(out_grad_all, contract_full), contract_low, CONTRACT_LAST, preferred_element_type=fl_type
    )
    gate_grad = hidden_grad * up * gate_sig * (1.0 + gate * (1.0 - gate_sig))
    up_grad = hidden_grad * gate_act
    gate_grad, up_grad = gate_grad.astype(bf_type), up_grad.astype(bf_type)
    gate_full = lax.dot_general(
        normed_two_all, gate_grad, CONTRACT_FIRST, preferred_element_type=fl_type
    ).astype(bf_type)
    up_full = lax.dot_general(
        after(normed_two_all, gate_full), up_grad, CONTRACT_FIRST, preferred_element_type=fl_type
    ).astype(bf_type)
    gate_reduced, up_reduced = reduce_columns(gate_full), reduce_columns(up_full)
    gate_up_grad = after(jnp.concatenate([gate_grad, up_grad], axis=1), up_full)
    normed_two_grad = scatter_tokens(
        lax.dot_general(gate_up_grad, expand_low, CONTRACT_LAST, preferred_element_type=fl_type)
    )
    middle_pull = jax.vjp(normalize, middle, gain_rows[1])[1]
    middle_part, gain_two_grad = middle_pull(normed_two_grad)
    middle_grad = out_grad + middle_part
    attended_all = gather_tokens(middle_grad.astype(bf_type))
    branch = scatter_tokens(
        jnp.dot(after(hidden, middle_grad), contract_low, preferred_element_type=fl_type)
    )
    layer_output = (middle + branch).astype(bf_type)
    mixing_full = lax.dot_general(
        mixed, attended_all, CONTRACT_FIRST, preferred_element_type=fl_type
    ).astype(bf_type)
    mixing_reduced = reduce_owned(mixing_full)
    attended_all = after(attended_all, mixing_full, contract_reduced)
    contract_grad = scatter_owned(contract_reduced)
    mixed_grad = (
        lax.dot_general(attended_all, mixing_low, CONTRACT_LAST, preferred_element_type=fl_type)
        .astype(bf_type)
        .reshape(token_count, head_count, HEAD_DIM)
    )
    query_grads = []
    key_grads = []
    value_grads = []
    for group_index in range(2):
        for kv_index in range(kv_count):
            query_block, key_block, masked = head_scores(group_index, kv_index)
            soft_exact = jnp.exp(masked - log_totals[group_index, kv_index])
            out_block = part(mixed_grad, group_index, kv_index, group_ratio)
            prob_grad = jnp.einsum(
                "gre,ke->rgk",
                out_block,
                part(values, group_index, kv_index, 1)[:, 0],
                preferred_element_type=fl_type,
            )
            inner_sum = jnp.sum(prob_grad * soft_exact, axis=-1, keepdims=True)
            score_grad = (soft_exact * (prob_grad - inner_sum)).astype(bf_type)
            query_grads.append(
                jnp.einsum("rgk,ke->gre", score_grad, key_block, preferred_element_type=fl_type)
                * factor
            )
            key_grads.append(
                jnp.einsum("rgk,gre->ke", score_grad, query_block, preferred_element_type=fl_type)
                * factor
            )
            value_grads.append(
                jnp.einsum(
                    "rgk,gre->ke",
                    soft_exact.astype(bf_type),
                    out_block,
                    preferred_element_type=fl_type,
                )
            )

    def assemble(blocks, axis):
        return jnp.concatenate(
            [
                jnp.concatenate(blocks[:kv_count], axis=axis),
                jnp.concatenate(blocks[kv_count:], axis=axis),
            ]
        )

    query_back = (
        rotate(assemble(query_grads, 1), cosine_table, -sine_table)
        .astype(bf_type)
        .reshape(token_count, query_width)
    )
    key_back = rotate(
        assemble(key_grads, 1).reshape(token_count, kv_count, HEAD_DIM), cosine_table, -sine_table
    ).reshape(token_count, key_width)
    value_back = assemble(value_grads, 1)
    qkv_back = jnp.concatenate(
        [query_back, key_back.astype(bf_type), value_back.astype(bf_type)], axis=1
    )
    qkv_back = after(qkv_back, gate_reduced)
    qkv_full = lax.dot_general(
        normed_all, qkv_back, CONTRACT_FIRST, preferred_element_type=fl_type
    ).astype(bf_type)
    qkv_reduced = reduce_columns(qkv_full)
    qkv_back = after(qkv_back, qkv_full, up_reduced, contract_grad)
    expand_parts = scatter_columns(gate_reduced) + scatter_columns(up_reduced)
    mixing_grad = scatter_owned(after(mixing_reduced, qkv_back))
    qkv_parts = scatter_columns(after(qkv_reduced, qkv_back))
    normed_grad = scatter_tokens(
        lax.dot_general(qkv_back, qkv_low, CONTRACT_LAST, preferred_element_type=fl_type)
    )
    rows_pull = jax.vjp(normalize, input_rows, gain_rows[0])[1]
    rows_part, gain_one_grad = rows_pull(normed_grad)
    input_grad = middle_grad + rows_part
    gain_parts = jnp.stack([gain_one_grad, gain_two_grad]).reshape(2, 2 * dp_count, -1)
    gain_sums = jnp.sum(
        lax.all_to_all(gain_parts, ("dp", "tensor"), split_axis=1, concat_axis=1, tiled=True),
        axis=1,
    )
    (
        (query_master, query_momentum, query_variance, query_average),
        (keyval_master, keyval_momentum, keyval_variance, keyval_average),
    ) = projection_update(
        qkv_parts,
        pair_bit,
        [query_weight, query_moment, query_second, query_shadow],
        [keyval_weight, keyval_moment, keyval_second, keyval_shadow],
    )
    mixing_master, mixing_momentum, mixing_variance, mixing_average = adamw(
        mixing_grad,
        mixing_weight,
        mixing_moment,
        mixing_second,
        mixing_shadow,
        MATRIX_RATE,
        WEIGHT_DECAY,
        EMA_KEEP,
    )
    expand_master, expand_momentum, expand_variance, expand_average = expand_update(
        expand_parts, pair_bit, expand_weight, expand_moment, expand_second, expand_shadow
    )
    contract_master, contract_momentum, contract_variance, contract_average = adamw(
        contract_grad,
        contract_weight,
        contract_moment,
        contract_second,
        contract_shadow,
        MATRIX_RATE,
        WEIGHT_DECAY,
        EMA_KEEP,
    )
    norms_master, norms_momentum, norms_variance, norms_average = adamw(
        gain_sums, norms_weight, norms_moment, norms_second, norms_shadow, GAIN_RATE, 0.0, GAIN_KEEP
    )
    return (
        layer_output,
        input_grad,
        query_master,
        query_momentum,
        query_variance,
        query_average,
        keyval_master,
        keyval_momentum,
        keyval_variance,
        keyval_average,
        mixing_master,
        mixing_momentum,
        mixing_variance,
        mixing_average,
        expand_master,
        expand_momentum,
        expand_variance,
        expand_average,
        contract_master,
        contract_momentum,
        contract_variance,
        contract_average,
        norms_master,
        norms_momentum,
        norms_variance,
        norms_average,
    )


def solution(mesh):
    in_specs = (
        P(("dp", "tensor"), None),
        P(("dp", "tensor"), None),
        P("dp", None),
        P("dp", None),
        P("dp", "tensor"),
        P("dp", "tensor"),
        P("dp", "tensor"),
        P("dp", "tensor"),
        P("dp", None, "tensor"),
        P("dp", None, "tensor"),
        P("dp", None, "tensor"),
        P("dp", None, "tensor"),
        P(("tensor", "dp"), None),
        P(("tensor", "dp"), None),
        P(("tensor", "dp"), None),
        P(("tensor", "dp"), None),
        P("dp", None, "tensor"),
        P("dp", None, "tensor"),
        P("dp", None, "tensor"),
        P("dp", None, "tensor"),
        P(("tensor", "dp"), None),
        P(("tensor", "dp"), None),
        P(("tensor", "dp"), None),
        P(("tensor", "dp"), None),
        P(None, ("dp", "tensor")),
        P(None, ("dp", "tensor")),
        P(None, ("dp", "tensor")),
        P(None, ("dp", "tensor")),
    )
    out_specs = (
        P(("dp", "tensor"), None),
        P(("dp", "tensor"), None),
        P("dp", "tensor"),
        P("dp", "tensor"),
        P("dp", "tensor"),
        P("dp", "tensor"),
        P("dp", None, "tensor"),
        P("dp", None, "tensor"),
        P("dp", None, "tensor"),
        P("dp", None, "tensor"),
        P(("tensor", "dp"), None),
        P(("tensor", "dp"), None),
        P(("tensor", "dp"), None),
        P(("tensor", "dp"), None),
        P("dp", None, "tensor"),
        P("dp", None, "tensor"),
        P("dp", None, "tensor"),
        P("dp", None, "tensor"),
        P(("tensor", "dp"), None),
        P(("tensor", "dp"), None),
        P(("tensor", "dp"), None),
        P(("tensor", "dp"), None),
        P(None, ("dp", "tensor")),
        P(None, ("dp", "tensor")),
        P(None, ("dp", "tensor")),
        P(None, ("dp", "tensor")),
    )
    return jax.shard_map(
        per_device, mesh=mesh, in_specs=in_specs, out_specs=out_specs, check_vma=False
    )
```

```python
import jax
import jax.numpy as jnp
from jax import lax
from jax.experimental import pallas as pl
from jax.experimental.pallas import tpu as pltpu
from jax.sharding import PartitionSpec as P

HEAD_DIM = 64
STEP = 5


NORM_EPS = 1e-05
NEG_FILL = -1e30
ROPE_BASE = 10000.0
BETA_ONE = 0.5
BETA_TWO = 0.5
ADAM_EPS = 1e-08
WEIGHT_DECAY = 0.1
MATRIX_RATE = 0.02
GAIN_RATE = 0.2
EMA_KEEP = 0.9
GAIN_KEEP = 0.5
CONTRACT_LAST = (((1,), (1,)), ((), ()))
CONTRACT_FIRST = (((0,), (0,)), ((), ()))


def normalize(field_rows, gain_row):
    factor = lax.rsqrt(jnp.mean(field_rows * field_rows, axis=-1, keepdims=True) + NORM_EPS)
    return field_rows * factor * gain_row


def rotate(field, cosine_table, sine_table):
    half_dim = field.shape[-1] // 2
    first_half = field[..., :half_dim]
    second_half = field[..., half_dim:]
    return jnp.concatenate(
        [
            first_half * cosine_table - second_half * sine_table,
            second_half * cosine_table + first_half * sine_table,
        ],
        axis=-1,
    )


def layout(lengths, valid_keys, places):
    doc_ends = jnp.cumsum(lengths)
    doc_starts = doc_ends - lengths
    segment = jnp.sum((doc_ends[None, :] <= places[:, None]).astype(jnp.int32), axis=1)
    owned_doc = segment[:, None] == jnp.arange(lengths.shape[0], dtype=jnp.int32)[None, :]
    position = places - jnp.sum(jnp.where(owned_doc, doc_starts[None, :], 0), axis=1)
    allowed = (
        (segment[:, None] == segment[None, :])
        & (places[None, :] <= places[:, None])
        & ((valid_keys[None, :] == 1) | (places[:, None] == places[None, :]))
    )
    return (position, allowed)


def rope_tables(position, head_size):
    half_dim = head_size // 2
    inverse = ROPE_BASE ** (-(2.0 * jnp.arange(half_dim, dtype=jnp.float32)) / head_size)
    angles = position.astype(jnp.float32)[:, None] * inverse[None, :]
    return (jnp.cos(angles)[:, None, :], jnp.sin(angles)[:, None, :])


def adamw(grad_value, weight, moment, second, shadow, step_rate, decay_rate, keep_rate):
    moment_new = BETA_ONE * moment + (1.0 - BETA_ONE) * grad_value
    second_new = BETA_TWO * second + (1.0 - BETA_TWO) * grad_value * grad_value
    moment_hat = moment_new / (1.0 - BETA_ONE**STEP)
    second_hat = second_new / (1.0 - BETA_TWO**STEP)
    weight_new = weight - step_rate * (
        moment_hat / (jnp.sqrt(second_hat) + ADAM_EPS) + decay_rate * weight
    )
    shadow_new = keep_rate * shadow + (1.0 - keep_rate) * weight_new
    return (weight_new, moment_new, second_new, shadow_new)


def chunks_of(width):
    first = width // 256 * 128
    return ((0, first), (first, width - first))


def cast_chunks(weight, pair_bit):
    row_count, planes, columns = weight.shape
    half = columns // 2
    chunks = chunks_of(half)

    def kernel(bit_ref, weight_ref, keep_ref, send_ref, last_ref):
        mine = bit_ref[0] == 0
        for number, (start, width) in enumerate(chunks):
            for plane in range(planes):
                low, high = [
                    weight_ref[:, plane, pl.ds(side * half + start, width)].astype(jnp.bfloat16)
                    for side in range(2)
                ]
                at = pl.ds(plane * width, width)
                if number == 0:
                    keep_ref[:, at] = jnp.where(mine, low, high)
                    send_ref[:, at] = jnp.where(mine, high, low)
                else:
                    for outer in range(2):
                        last_ref[2 * outer, :, at] = low
                        last_ref[2 * outer + 1, :, at] = high

    first, last = [planes * width for _, width in chunks]
    step = 32
    rows = pl.BlockSpec((step, first), lambda i, bit: (i, 0))
    keep, send, blocks = pl.pallas_call(
        kernel,
        grid_spec=pltpu.PrefetchScalarGridSpec(
            num_scalar_prefetch=1,
            grid=(row_count // step,),
            in_specs=[pl.BlockSpec((step, planes, columns), lambda i, bit: (i, 0, 0))],
            out_specs=[rows, rows, pl.BlockSpec((4, step, last), lambda i, bit: (0, i, 0))],
        ),
        out_shape=[
            jax.ShapeDtypeStruct((row_count, first), jnp.bfloat16),
            jax.ShapeDtypeStruct((row_count, first), jnp.bfloat16),
            jax.ShapeDtypeStruct((4, row_count, last), jnp.bfloat16),
        ],
        compiler_params=pltpu.CompilerParams(vmem_limit_bytes=32 * 2**20),
    )(pair_bit.reshape(1), weight)
    return (keep, send), blocks


def join_low(blocks, low_index):
    parts, rows, columns = blocks[0].shape
    count = len(blocks)

    def kernel(low_ref, *refs):
        for flip in range(count):
            refs[count][0, low_ref[0] ^ flip] = refs[flip][0]

    return pl.pallas_call(
        kernel,
        grid_spec=pltpu.PrefetchScalarGridSpec(
            num_scalar_prefetch=1,
            grid=(parts,),
            in_specs=[pl.BlockSpec((1, rows, columns), lambda i, low: (i, 0, 0))] * count,
            out_specs=pl.BlockSpec((1, count, rows, columns), lambda i, low: (i, 0, 0, 0)),
        ),
        out_shape=jax.ShapeDtypeStruct((parts, count, rows, columns), blocks[0].dtype),
        compiler_params=pltpu.CompilerParams(vmem_limit_bytes=32 * 2**20),
    )(low_index.reshape(1), *blocks)


def cast_projections(query, keyval):
    row_count, columns = query.shape
    half, width = columns // 2, keyval.shape[2]

    def kernel(query_ref, keyval_ref, out_ref):
        left = lax.broadcasted_iota(jnp.int32, (row_count, width), 1) < width // 2
        key, value = keyval_ref[:, 0, :], keyval_ref[:, 1, :]
        pairs = (
            jnp.where(left, key, pltpu.roll(value, width // 2, 1)).astype(jnp.bfloat16),
            jnp.where(left, pltpu.roll(key, width // 2, 1), value).astype(jnp.bfloat16),
        )
        for place in range(4):
            side = place % 2
            part = query_ref[:, pl.ds(side * half, half)]
            out_ref[place, :, :half] = part.astype(jnp.bfloat16)
            out_ref[place, :, half:] = pairs[side]

    return pl.pallas_call(
        kernel,
        in_specs=[pl.BlockSpec(memory_space=pltpu.VMEM)] * 2,
        out_specs=pl.BlockSpec(memory_space=pltpu.VMEM),
        out_shape=jax.ShapeDtypeStruct((4, row_count, half + width), jnp.bfloat16),
        compiler_params=pltpu.CompilerParams(vmem_limit_bytes=16 * 2**20),
    )(query, keyval)


def projection_update(parts, pair_bit, queries, keyvals):
    row_count, columns = queries[0].shape
    half, width = columns // 2, keyvals[0].shape[2]

    def kernel(bit_ref, *refs):
        parts, olds, news = refs[:4], refs[4:12], refs[12:]
        one, two, three, four = [ref[...].astype(jnp.float32) for ref in parts]
        own, other = one + two, three + four
        mine = bit_ref[0] == 0
        low, high = jnp.where(mine, own, other), jnp.where(mine, other, own)
        left = lax.broadcasted_iota(jnp.int32, (row_count, width), 1) < width // 2
        low_pair, high_pair = low[:, half:], high[:, half:]
        grads = (
            (0, (slice(None), slice(0, half)), low[:, :half]),
            (0, (slice(None), slice(half, columns)), high[:, :half]),
            (4, (slice(None), 0), jnp.where(left, low_pair, pltpu.roll(high_pair, width // 2, 1))),
            (4, (slice(None), 1), jnp.where(left, pltpu.roll(low_pair, width // 2, 1), high_pair)),
        )
        for first, where, grad in grads:
            results = adamw(
                grad,
                *[ref[where] for ref in olds[first : first + 4]],
                MATRIX_RATE,
                WEIGHT_DECAY,
                EMA_KEEP,
            )
            for ref, result in zip(news[first : first + 4], results):
                ref[where] = result

    outs = [jax.ShapeDtypeStruct(old.shape, jnp.float32) for old in queries + keyvals]
    results = pl.pallas_call(
        kernel,
        in_specs=[pl.BlockSpec(memory_space=pltpu.SMEM)]
        + [pl.BlockSpec(memory_space=pltpu.VMEM)] * 12,
        out_specs=[pl.BlockSpec(memory_space=pltpu.VMEM)] * 8,
        out_shape=outs,
        compiler_params=pltpu.CompilerParams(vmem_limit_bytes=32 * 2**20),
    )(pair_bit.reshape(1), *parts, *queries, *keyvals)
    return results[:4], results[4:]


def expand_update(parts, olds):
    row_count, planes, columns = olds[0].shape
    half = columns // 2
    chunks = chunks_of(half)
    step = 16

    def kernel(*refs):
        part_refs, old_refs, new_refs = refs[:2], refs[2:6], refs[6:]
        for (start, width), part_ref in zip(chunks, part_refs):
            for plane in range(planes):
                at = pl.ds(plane * width, width)
                for side in range(2):
                    where = (slice(None), plane, pl.ds(side * half + start, width))
                    results = adamw(
                        part_ref[side, :, at].astype(jnp.float32)
                        + part_ref[side + 2, :, at].astype(jnp.float32),
                        *[ref[where] for ref in old_refs],
                        MATRIX_RATE,
                        WEIGHT_DECAY,
                        EMA_KEEP,
                    )
                    for ref, result in zip(new_refs, results):
                        ref[where] = result

    def state_spec():
        return pl.BlockSpec((step, planes, columns), lambda i: (i, 0, 0))

    out = jax.ShapeDtypeStruct(olds[0].shape, jnp.float32)
    return pl.pallas_call(
        kernel,
        grid=(row_count // step,),
        in_specs=[
            pl.BlockSpec((4, step, planes * width), lambda i: (0, i, 0)) for _, width in chunks
        ]
        + [state_spec() for _ in range(4)],
        out_specs=[state_spec() for _ in range(4)],
        out_shape=(out,) * 4,
        compiler_params=pltpu.CompilerParams(vmem_limit_bytes=48 * 2**20),
    )(*parts, *olds)


def per_device(
    layer_input,
    upstream,
    doc_lengths,
    token_valid,
    query_weight,
    query_moment,
    query_second,
    query_shadow,
    keyval_weight,
    keyval_moment,
    keyval_second,
    keyval_shadow,
    mixing_weight,
    mixing_moment,
    mixing_second,
    mixing_shadow,
    expand_weight,
    expand_moment,
    expand_second,
    expand_shadow,
    contract_weight,
    contract_moment,
    contract_second,
    contract_shadow,
    norms_weight,
    norms_moment,
    norms_second,
    norms_shadow,
):
    bf_type = jnp.bfloat16
    fl_type = jnp.float32
    dp_count = lax.axis_size("dp")
    low_count = dp_count // 4
    dp_index = lax.axis_index("dp")
    outer_bit = dp_index // (2 * low_count)
    pair_bit = (dp_index // low_count) % 2
    low_index = dp_index % low_count
    core_bit = lax.axis_index("tensor")
    low_groups = [[base * low_count + low for low in range(low_count)] for base in range(4)]

    def move(value, target):
        return lax.ppermute(
            value,
            "dp",
            [
                (place * low_count + low, goal * low_count + low)
                for place, goal in target.items()
                for low in range(low_count)
            ],
        )

    place_groups = [
        [place * low_count + low for place in range(4)] for low in range(low_count)
    ]

    def spread(blocks):
        return lax.all_to_all(
            blocks, "dp", split_axis=0, concat_axis=0, tiled=True, axis_index_groups=place_groups
        )

    def swap(value, flip):
        return move(value, {place: place ^ flip for place in range(4)})

    def swap_low(value, flip):
        return lax.ppermute(value, "dp", [(index, index ^ flip) for index in range(dp_count)])

    def swap_pair(value):
        return swap(value, 1)

    def swap_core(value):
        return lax.ppermute(value, "tensor", [(0, 1), (1, 0)])

    def after(value, *earlier):
        return lax.optimization_barrier((value,) + earlier)[0]

    def pick(bit, zero, one):
        return jnp.where(bit == 0, zero, one)

    def gather_low(blocks):
        return lax.all_gather(blocks, "dp", axis=1, tiled=True, axis_index_groups=low_groups)

    def scatter_low(blocks):
        return lax.psum_scatter(
            blocks, "dp", scatter_dimension=1, tiled=True, axis_index_groups=low_groups
        )

    own_rows, model_width = query_weight.shape[0], norms_weight.shape[1] * dp_count * 2

    def exchange_columns(keep, send):
        return keep, swap(send, 1), swap(keep, 2), swap(send, 3)

    def join_columns(keep, one, two, three):
        low_pair = [pick(pair_bit, keep, one), pick(pair_bit, one, keep)]
        high_pair = [pick(pair_bit, two, three), pick(pair_bit, three, two)]
        return pick(outer_bit, jnp.stack(low_pair + high_pair), jnp.stack(high_pair + low_pair))

    def exchange_owned(rows):
        return rows, move(rows, {0: 2, 1: 0, 2: 3, 3: 1}), move(rows, {1: 2, 2: 1})

    def join_owned(rows, first, second):
        second = pick(outer_bit ^ pair_bit, rows, second)
        return pick(outer_bit, jnp.stack([second, first]), jnp.stack([first, second]))

    def flat(blocks):
        return blocks.reshape(-1, blocks.shape[-1])

    def exchange_low(blocks):
        return [blocks] + [swap_low(blocks, flip) for flip in range(1, low_count)]

    def gather_direct(moved):
        return flat(join_low(moved, low_index))

    def low_blocks(full, parts):
        blocks = full.reshape(parts, low_count, -1, full.shape[1])
        return [
            lax.dynamic_index_in_dim(blocks, low_index ^ flip, 1, keepdims=False)
            for flip in range(low_count)
        ]

    def sent_low(blocks):
        return [swap_low(block, flip) if flip else block for flip, block in enumerate(blocks)]

    def total_low(terms):
        return sum(term.astype(fl_type) for term in terms).astype(bf_type)

    def columns_moved(reduced):
        place = 2 * outer_bit + pair_bit
        kept, one, two, three = [
            lax.dynamic_index_in_dim(reduced, place ^ flip, 0, keepdims=False) for flip in range(4)
        ]
        return kept, swap(two, 2), swap(one, 1), swap(three, 3)

    def gather_tokens(rows):
        away = swap_pair(rows)
        return jnp.concatenate([rows, swap_core(rows), away, swap_core(away)])

    def token_sums(partial, hold=()):
        own, across, away, far = jnp.split(partial, 4)

        def over_cores(mine, sent):
            return mine + swap_core(sent.astype(bf_type)).astype(fl_type)

        return over_cores(own, across), after(over_cores(away, far).astype(bf_type), *hold)

    def scatter_tokens(partial, fill=lambda: (), hold=()):
        kept, sent = token_sums(partial, hold)
        return kept + after(swap_pair(sent), *fill()).astype(fl_type)

    group_len = token_valid.shape[1]
    doc_count = doc_lengths.shape[1]
    gain_count = norms_weight.size
    first_rows, last_blocks = cast_chunks(expand_weight, pair_bit)
    first_moved = exchange_columns(*first_rows)
    mixing_moved = exchange_owned(after(mixing_weight, first_rows[0]).astype(bf_type))
    own_facts = jnp.concatenate(
        [
            norms_weight.reshape(-1),
            doc_lengths[0].astype(fl_type),
            token_valid[0].astype(fl_type),
        ]
    )
    facts = lax.all_to_all(
        jnp.broadcast_to(
            own_facts[None], (2 * dp_count, own_facts.size)
        ),
        ("dp", "tensor"),
        split_axis=0,
        concat_axis=0,
        tiled=True,
    )
    gain_rows = facts[:, :gain_count].reshape(2 * dp_count, 2, -1).transpose(1, 0, 2)
    gain_rows = gain_rows.reshape(2, model_width)
    partner = 2 * (dp_index ^ low_count) + core_bit
    partner_facts = lax.dynamic_index_in_dim(facts, partner, 0, keepdims=False)[gain_count:]
    partner_facts = partner_facts.astype(jnp.int32)
    other_lengths, other_valid = partner_facts[:doc_count], partner_facts[doc_count:]
    input_rows = layer_input.astype(fl_type)
    normed = normalize(input_rows, gain_rows[0]).astype(bf_type)
    normed_all = gather_tokens(normed)
    qkv_quad = spread(after(cast_projections(query_weight, keyval_weight), normed))
    qkv_moved = exchange_low(after(qkv_quad, normed))
    first_low = flat(gather_low(join_columns(*after(first_moved, normed))))
    mixing_both = join_owned(*mixing_moved)
    last_quad = spread(after(last_blocks, mixing_both, qkv_quad))
    contract_moved = exchange_owned(after(contract_weight, last_quad).astype(bf_type))
    qkv_low = gather_direct(after(qkv_moved, mixing_both))
    mixing_low = gather_direct(exchange_low(after(mixing_both, qkv_low)))
    last_low = flat(gather_low(after(last_quad, normed_all)))
    contract_both = join_owned(*contract_moved)
    contract_low = flat(gather_low(contract_both))
    out_grad_all = gather_tokens(after(upstream, normed_all))
    places = (
        jnp.arange(group_len, dtype=jnp.int32) + core_bit * (group_len // 2)
    ) % group_len

    def ordered_valid(valid):
        first, second = valid[: group_len // 2], valid[group_len // 2 :]
        return pick(
            core_bit, jnp.concatenate([first, second]), jnp.concatenate([second, first])
        )

    position_one, allowed_one = layout(doc_lengths[0], ordered_valid(token_valid[0]), places)
    position_two, allowed_two = layout(other_lengths, ordered_valid(other_valid), places)
    allowed = (allowed_one, allowed_two)
    cosine_table, sine_table = rope_tables(
        jnp.concatenate([position_one, position_two]), HEAD_DIM
    )
    token_count = 2 * group_len
    query_width = query_weight.shape[1] // 2
    key_width = keyval_weight.shape[2] // 2
    head_count = query_width // HEAD_DIM
    kv_count = key_width // HEAD_DIM
    group_ratio = head_count // kv_count
    hidden_width = expand_weight.shape[2] // 2
    factor = HEAD_DIM ** (-0.5)
    qkv_pre = jnp.dot(normed_all, qkv_low, preferred_element_type=fl_type)
    queries = rotate(
        qkv_pre[:, :query_width].reshape(token_count, head_count, HEAD_DIM),
        cosine_table,
        sine_table,
    ).astype(bf_type)
    keys = rotate(
        qkv_pre[:, query_width : query_width + key_width].reshape(token_count, kv_count, HEAD_DIM),
        cosine_table,
        sine_table,
    ).astype(bf_type)
    values = (
        qkv_pre[:, query_width + key_width :]
        .reshape(token_count, kv_count, HEAD_DIM)
        .astype(bf_type)
    )


    def part(array, group_index, kv_index, heads):
        return array[
            group_index * group_len : (group_index + 1) * group_len,
            kv_index * heads : (kv_index + 1) * heads,
        ]

    def head_scores(group_index, kv_index):
        query_block = part(queries, group_index, kv_index, group_ratio)
        key_block = part(keys, group_index, kv_index, 1)[:, 0]
        raw_scores = (
            jnp.einsum("gre,ke->rgk", query_block, key_block, preferred_element_type=fl_type)
            * factor
        )
        return (query_block, key_block, jnp.where(allowed[group_index][None], raw_scores, NEG_FILL))

    mixed_groups = []
    log_totals = {}
    for group_index in range(2):
        mixed_parts = []
        for kv_index in range(kv_count):
            _, _, masked = head_scores(group_index, kv_index)
            largest = jnp.max(masked, axis=-1, keepdims=True)
            exp_scores = jnp.exp(masked - largest)
            totals = jnp.sum(exp_scores, axis=-1, keepdims=True)
            soft_probs = (exp_scores / totals).astype(bf_type)
            log_totals[group_index, kv_index] = largest + jnp.log(totals)
            mixed_parts.append(
                jnp.einsum(
                    "rgk,ke->gre",
                    soft_probs,
                    part(values, group_index, kv_index, 1)[:, 0],
                    preferred_element_type=fl_type,
                )
            )
        mixed_groups.append(jnp.concatenate(mixed_parts, axis=1))
    mixed = jnp.concatenate(mixed_groups).reshape(token_count, query_width).astype(bf_type)
    attended = scatter_tokens(
        jnp.dot(
            after(mixed, contract_both, out_grad_all), mixing_low, preferred_element_type=fl_type
        )
    )
    middle = input_rows + attended
    normed_two = normalize(middle, gain_rows[1]).astype(bf_type)
    normed_two_all = gather_tokens(normed_two)
    def gated(rows, weights):
        gate_up = jnp.dot(rows, weights, preferred_element_type=fl_type)
        return jnp.split(gate_up, 2, axis=1)

    gate_first, up_first = gated(normed_two_all, first_low)
    gate_last, up_last = gated(after(normed_two_all, gate_first), last_low)
    hidden = jnp.concatenate(
        [
            (jax.nn.silu(gate) * up).astype(bf_type)
            for gate, up in ((gate_first, up_first), (gate_last, up_last))
        ],
        axis=1,
    )
    out_grad = upstream.astype(fl_type)

    def reduce_columns(full):
        return scatter_low(full.reshape(4, low_count * own_rows, full.shape[1]))

    def reduce_owned(full):
        return scatter_low(full.reshape(2, full.shape[0] // 2, full.shape[1]))

    def owned_sent(reduced):
        rest = pick(outer_bit, reduced[0], reduced[1])
        first = move(pick(outer_bit, reduced[1], reduced[0]), {0: 1, 1: 3, 2: 0, 3: 2})
        return first, rest, move(rest, {1: 2, 2: 1})

    def owned_total(first, rest, second):
        return first.astype(fl_type) + pick(outer_bit ^ pair_bit, rest, second).astype(fl_type)

    contract_full = lax.dot_general(
        hidden, out_grad_all, CONTRACT_FIRST, preferred_element_type=fl_type
    ).astype(bf_type)
    contract_reduced = reduce_owned(contract_full)
    hidden_grad = lax.dot_general(
        after(out_grad_all, contract_full), contract_low, CONTRACT_LAST, preferred_element_type=fl_type
    )

    def gated_grad(gate, up, grad):
        gate_sig = jax.nn.sigmoid(gate)
        gate_grad = grad * up * gate_sig * (1.0 + gate * (1.0 - gate_sig))
        up_grad = grad * (gate * gate_sig)
        return jnp.concatenate([gate_grad.astype(bf_type), up_grad.astype(bf_type)], axis=1)

    first_width = first_low.shape[1] // 2
    first_grad = gated_grad(gate_first, up_first, hidden_grad[:, :first_width])
    last_grad = gated_grad(gate_last, up_last, hidden_grad[:, first_width:])
    last_full = lax.dot_general(
        normed_two_all, last_grad, CONTRACT_FIRST, preferred_element_type=fl_type
    ).astype(bf_type)
    first_full = lax.dot_general(
        after(normed_two_all, last_full),
        first_grad,
        CONTRACT_FIRST,
        preferred_element_type=fl_type,
    ).astype(bf_type)
    last_reduced, first_reduced = reduce_columns(last_full), reduce_columns(first_full)
    normed_two_partial = lax.dot_general(
        after(last_grad, first_full), last_low, CONTRACT_LAST, preferred_element_type=fl_type
    ) + lax.dot_general(first_grad, first_low, CONTRACT_LAST, preferred_element_type=fl_type)
    branch_partial = jnp.dot(
        after(hidden, normed_two_partial), contract_low, preferred_element_type=fl_type
    )
    normed_two_grad = scatter_tokens(normed_two_partial, lambda: (branch_partial,))
    middle_pull = jax.vjp(normalize, middle, gain_rows[1])[1]
    middle_part, gain_two_grad = middle_pull(normed_two_grad)
    middle_grad = out_grad + middle_part
    attended_all = gather_tokens(middle_grad.astype(bf_type))
    contract_sent = owned_sent(after(contract_reduced, middle_grad))
    mixing_full = lax.dot_general(
        mixed, attended_all, CONTRACT_FIRST, preferred_element_type=fl_type
    ).astype(bf_type)
    mixing_reduced = reduce_owned(mixing_full)
    attended_all = after(attended_all, mixing_full)
    mixed_grad = (
        lax.dot_general(attended_all, mixing_low, CONTRACT_LAST, preferred_element_type=fl_type)
        .astype(bf_type)
        .reshape(token_count, head_count, HEAD_DIM)
    )
    mixed_grad = after(mixed_grad, last_reduced)
    last_parts = spread(last_reduced)
    query_grads = []
    key_grads = []
    value_grads = []
    for group_index in range(2):
        if group_index == 1:
            mixed_grad = after(mixed_grad, query_grads[0], *contract_sent)
        for kv_index in range(kv_count):
            query_block, key_block, masked = head_scores(group_index, kv_index)
            soft_exact = jnp.exp(masked - log_totals[group_index, kv_index])
            out_block = part(mixed_grad, group_index, kv_index, group_ratio)
            prob_grad = jnp.einsum(
                "gre,ke->rgk",
                out_block,
                part(values, group_index, kv_index, 1)[:, 0],
                preferred_element_type=fl_type,
            )
            inner_sum = jnp.sum(prob_grad * soft_exact, axis=-1, keepdims=True)
            score_grad = (soft_exact * (prob_grad - inner_sum)).astype(bf_type)
            if group_index == 1:
                score_grad = after(score_grad, last_parts)
            query_grads.append(
                jnp.einsum("rgk,ke->gre", score_grad, key_block, preferred_element_type=fl_type)
                * factor
            )
            key_grads.append(
                jnp.einsum("rgk,gre->ke", score_grad, query_block, preferred_element_type=fl_type)
                * factor
            )
            value_grads.append(
                jnp.einsum(
                    "rgk,gre->ke",
                    soft_exact.astype(bf_type),
                    out_block,
                    preferred_element_type=fl_type,
                )
            )

    def assemble(blocks, axis):
        return jnp.concatenate(
            [
                jnp.concatenate(blocks[:kv_count], axis=axis),
                jnp.concatenate(blocks[kv_count:], axis=axis),
            ]
        )

    query_back = (
        rotate(assemble(query_grads, 1), cosine_table, -sine_table)
        .astype(bf_type)
        .reshape(token_count, query_width)
    )
    key_back = rotate(
        assemble(key_grads, 1).reshape(token_count, kv_count, HEAD_DIM), cosine_table, -sine_table
    ).reshape(token_count, key_width)
    value_back = assemble(value_grads, 1)
    qkv_back = jnp.concatenate(
        [query_back, key_back.astype(bf_type), value_back.astype(bf_type)], axis=1
    )
    expand_states = [expand_weight, expand_moment, expand_second, expand_shadow]
    branch = scatter_tokens(
        branch_partial, lambda: (query_grads[-1],), hold=(attended_all,)
    )
    layer_output = (middle + branch).astype(bf_type)
    contract_news = adamw(
        owned_total(*contract_sent),
        contract_weight,
        contract_moment,
        contract_second,
        contract_shadow,
        MATRIX_RATE,
        WEIGHT_DECAY,
        EMA_KEEP,
    )
    qkv_back = after(qkv_back, layer_output, last_parts)
    qkv_full = lax.dot_general(
        normed_all, qkv_back, CONTRACT_FIRST, preferred_element_type=fl_type
    ).astype(bf_type)
    qkv_blocks = low_blocks(qkv_full, 4)
    qkv_moved = sent_low(qkv_blocks)
    normed_partial = lax.dot_general(
        after(qkv_back, *qkv_blocks), qkv_low, CONTRACT_LAST, preferred_element_type=fl_type
    )
    first_parts = spread(after(first_reduced, normed_partial))
    normed_kept, normed_sent = token_sums(normed_partial)
    normed_away = swap_pair(normed_sent)
    qkv_total = total_low(after(qkv_moved, normed_sent))
    normed_away = after(normed_away, first_parts, qkv_total, *contract_news)
    normed_grad = normed_kept + normed_away.astype(fl_type)
    expand_news = expand_update((first_parts, last_parts), expand_states)
    qkv_parts = after(columns_moved(qkv_total), *expand_news)
    mixing_grad = owned_total(*owned_sent(after(mixing_reduced, first_parts)))
    rows_pull = jax.vjp(normalize, input_rows, gain_rows[0])[1]
    rows_part, gain_one_grad = rows_pull(normed_grad)
    input_grad = middle_grad + rows_part
    gain_parts = after(jnp.stack([gain_one_grad, gain_two_grad]), first_parts).reshape(2, 2 * dp_count, -1)
    gain_sums = jnp.sum(
        lax.all_to_all(gain_parts, ("dp", "tensor"), split_axis=1, concat_axis=1, tiled=True),
        axis=1,
    )
    (
        (query_master, query_momentum, query_variance, query_average),
        (keyval_master, keyval_momentum, keyval_variance, keyval_average),
    ) = projection_update(
        qkv_parts,
        pair_bit,
        [query_weight, query_moment, query_second, query_shadow],
        [keyval_weight, keyval_moment, keyval_second, keyval_shadow],
    )
    mixing_master, mixing_momentum, mixing_variance, mixing_average = adamw(
        mixing_grad,
        mixing_weight,
        mixing_moment,
        mixing_second,
        mixing_shadow,
        MATRIX_RATE,
        WEIGHT_DECAY,
        EMA_KEEP,
    )
    expand_master, expand_momentum, expand_variance, expand_average = expand_news
    contract_master, contract_momentum, contract_variance, contract_average = contract_news
    norms_master, norms_momentum, norms_variance, norms_average = adamw(
        gain_sums, norms_weight, norms_moment, norms_second, norms_shadow, GAIN_RATE, 0.0, GAIN_KEEP
    )
    return (
        layer_output,
        input_grad,
        query_master,
        query_momentum,
        query_variance,
        query_average,
        keyval_master,
        keyval_momentum,
        keyval_variance,
        keyval_average,
        mixing_master,
        mixing_momentum,
        mixing_variance,
        mixing_average,
        expand_master,
        expand_momentum,
        expand_variance,
        expand_average,
        contract_master,
        contract_momentum,
        contract_variance,
        contract_average,
        norms_master,
        norms_momentum,
        norms_variance,
        norms_average,
    )


def solution(mesh):
    in_specs = (
        P(("dp", "tensor"), None),
        P(("dp", "tensor"), None),
        P("dp", None),
        P("dp", None),
        P("dp", "tensor"),
        P("dp", "tensor"),
        P("dp", "tensor"),
        P("dp", "tensor"),
        P("dp", None, "tensor"),
        P("dp", None, "tensor"),
        P("dp", None, "tensor"),
        P("dp", None, "tensor"),
        P(("tensor", "dp"), None),
        P(("tensor", "dp"), None),
        P(("tensor", "dp"), None),
        P(("tensor", "dp"), None),
        P("dp", None, "tensor"),
        P("dp", None, "tensor"),
        P("dp", None, "tensor"),
        P("dp", None, "tensor"),
        P(("tensor", "dp"), None),
        P(("tensor", "dp"), None),
        P(("tensor", "dp"), None),
        P(("tensor", "dp"), None),
        P(None, ("dp", "tensor")),
        P(None, ("dp", "tensor")),
        P(None, ("dp", "tensor")),
        P(None, ("dp", "tensor")),
    )
    out_specs = (
        P(("dp", "tensor"), None),
        P(("dp", "tensor"), None),
        P("dp", "tensor"),
        P("dp", "tensor"),
        P("dp", "tensor"),
        P("dp", "tensor"),
        P("dp", None, "tensor"),
        P("dp", None, "tensor"),
        P("dp", None, "tensor"),
        P("dp", None, "tensor"),
        P(("tensor", "dp"), None),
        P(("tensor", "dp"), None),
        P(("tensor", "dp"), None),
        P(("tensor", "dp"), None),
        P("dp", None, "tensor"),
        P("dp", None, "tensor"),
        P("dp", None, "tensor"),
        P("dp", None, "tensor"),
        P(("tensor", "dp"), None),
        P(("tensor", "dp"), None),
        P(("tensor", "dp"), None),
        P(("tensor", "dp"), None),
        P(None, ("dp", "tensor")),
        P(None, ("dp", "tensor")),
        P(None, ("dp", "tensor")),
        P(None, ("dp", "tensor")),
    )
    return jax.shard_map(
        per_device, mesh=mesh, in_specs=in_specs, out_specs=out_specs, check_vma=False
    )
```

```python
import jax
import jax.numpy as jnp
from jax import lax
from jax.experimental import pallas as pl
from jax.experimental.pallas import tpu as pltpu
from jax.sharding import PartitionSpec as P

HEAD_DIM = 64
STEP = 5


NORM_EPS = 1e-05
NEG_FILL = -1e30
ROPE_BASE = 10000.0
BETA_ONE = 0.5
BETA_TWO = 0.5
ADAM_EPS = 1e-08
WEIGHT_DECAY = 0.1
MATRIX_RATE = 0.02
GAIN_RATE = 0.2
EMA_KEEP = 0.9
GAIN_KEEP = 0.5
CONTRACT_LAST = (((1,), (1,)), ((), ()))
CONTRACT_FIRST = (((0,), (0,)), ((), ()))


def normalize(field_rows, gain_row):
    factor = lax.rsqrt(jnp.mean(field_rows * field_rows, axis=-1, keepdims=True) + NORM_EPS)
    return field_rows * factor * gain_row


def rotate(field, cosine_table, sine_table):
    half_dim = field.shape[-1] // 2
    first_half = field[..., :half_dim]
    second_half = field[..., half_dim:]
    return jnp.concatenate(
        [
            first_half * cosine_table - second_half * sine_table,
            second_half * cosine_table + first_half * sine_table,
        ],
        axis=-1,
    )


def layout(lengths, valid_keys, places):
    doc_ends = jnp.cumsum(lengths)
    doc_starts = doc_ends - lengths
    segment = jnp.sum((doc_ends[None, :] <= places[:, None]).astype(jnp.int32), axis=1)
    owned_doc = segment[:, None] == jnp.arange(lengths.shape[0], dtype=jnp.int32)[None, :]
    position = places - jnp.sum(jnp.where(owned_doc, doc_starts[None, :], 0), axis=1)
    allowed = (
        (segment[:, None] == segment[None, :])
        & (places[None, :] <= places[:, None])
        & ((valid_keys[None, :] == 1) | (places[:, None] == places[None, :]))
    )
    return (position, allowed)


def rope_tables(position, head_size):
    half_dim = head_size // 2
    inverse = ROPE_BASE ** (-(2.0 * jnp.arange(half_dim, dtype=jnp.float32)) / head_size)
    angles = position.astype(jnp.float32)[:, None] * inverse[None, :]
    return (jnp.cos(angles)[:, None, :], jnp.sin(angles)[:, None, :])


def adamw(grad_value, weight, moment, second, shadow, step_rate, decay_rate, keep_rate):
    moment_new = BETA_ONE * moment + (1.0 - BETA_ONE) * grad_value
    second_new = BETA_TWO * second + (1.0 - BETA_TWO) * grad_value * grad_value
    moment_hat = moment_new / (1.0 - BETA_ONE**STEP)
    second_hat = second_new / (1.0 - BETA_TWO**STEP)
    weight_new = weight - step_rate * (
        moment_hat / (jnp.sqrt(second_hat) + ADAM_EPS) + decay_rate * weight
    )
    shadow_new = keep_rate * shadow + (1.0 - keep_rate) * weight_new
    return (weight_new, moment_new, second_new, shadow_new)


def chunks_of(width):
    first = width // 256 * 128
    return ((0, first), (first, width - first))


def cast_chunks(weight, pair_bit):
    row_count, planes, columns = weight.shape
    half = columns // 2
    chunks = chunks_of(half)

    def kernel(bit_ref, weight_ref, keep_ref, send_ref, last_ref):
        mine = bit_ref[0] == 0
        for number, (start, width) in enumerate(chunks):
            for plane in range(planes):
                low, high = [
                    weight_ref[:, plane, pl.ds(side * half + start, width)].astype(jnp.bfloat16)
                    for side in range(2)
                ]
                at = pl.ds(plane * width, width)
                if number == 0:
                    keep_ref[:, at] = jnp.where(mine, low, high)
                    send_ref[:, at] = jnp.where(mine, high, low)
                else:
                    for outer in range(2):
                        last_ref[2 * outer, :, at] = low
                        last_ref[2 * outer + 1, :, at] = high

    first, last = [planes * width for _, width in chunks]
    step = 32
    rows = pl.BlockSpec((step, first), lambda i, bit: (i, 0))
    keep, send, blocks = pl.pallas_call(
        kernel,
        grid_spec=pltpu.PrefetchScalarGridSpec(
            num_scalar_prefetch=1,
            grid=(row_count // step,),
            in_specs=[pl.BlockSpec((step, planes, columns), lambda i, bit: (i, 0, 0))],
            out_specs=[rows, rows, pl.BlockSpec((4, step, last), lambda i, bit: (0, i, 0))],
        ),
        out_shape=[
            jax.ShapeDtypeStruct((row_count, first), jnp.bfloat16),
            jax.ShapeDtypeStruct((row_count, first), jnp.bfloat16),
            jax.ShapeDtypeStruct((4, row_count, last), jnp.bfloat16),
        ],
        compiler_params=pltpu.CompilerParams(vmem_limit_bytes=32 * 2**20),
    )(pair_bit.reshape(1), weight)
    return (keep, send), blocks


def join_low(blocks, low_index):
    parts, rows, columns = blocks[0].shape
    count = len(blocks)

    def kernel(low_ref, *refs):
        for flip in range(count):
            refs[count][0, low_ref[0] ^ flip] = refs[flip][0]

    return pl.pallas_call(
        kernel,
        grid_spec=pltpu.PrefetchScalarGridSpec(
            num_scalar_prefetch=1,
            grid=(parts,),
            in_specs=[pl.BlockSpec((1, rows, columns), lambda i, low: (i, 0, 0))] * count,
            out_specs=pl.BlockSpec((1, count, rows, columns), lambda i, low: (i, 0, 0, 0)),
        ),
        out_shape=jax.ShapeDtypeStruct((parts, count, rows, columns), blocks[0].dtype),
        compiler_params=pltpu.CompilerParams(vmem_limit_bytes=32 * 2**20),
    )(low_index.reshape(1), *blocks)


def cast_projections(query, keyval):
    row_count, columns = query.shape
    half, width = columns // 2, keyval.shape[2]

    def kernel(query_ref, keyval_ref, out_ref):
        left = lax.broadcasted_iota(jnp.int32, (row_count, width), 1) < width // 2
        key, value = keyval_ref[:, 0, :], keyval_ref[:, 1, :]
        pairs = (
            jnp.where(left, key, pltpu.roll(value, width // 2, 1)).astype(jnp.bfloat16),
            jnp.where(left, pltpu.roll(key, width // 2, 1), value).astype(jnp.bfloat16),
        )
        for place in range(4):
            side = place % 2
            part = query_ref[:, pl.ds(side * half, half)]
            out_ref[place, :, :half] = part.astype(jnp.bfloat16)
            out_ref[place, :, half:] = pairs[side]

    return pl.pallas_call(
        kernel,
        in_specs=[pl.BlockSpec(memory_space=pltpu.VMEM)] * 2,
        out_specs=pl.BlockSpec(memory_space=pltpu.VMEM),
        out_shape=jax.ShapeDtypeStruct((4, row_count, half + width), jnp.bfloat16),
        compiler_params=pltpu.CompilerParams(vmem_limit_bytes=16 * 2**20),
    )(query, keyval)


def projection_update(parts, pair_bit, queries, keyvals):
    row_count, columns = queries[0].shape
    half, width = columns // 2, keyvals[0].shape[2]

    def kernel(bit_ref, *refs):
        parts, olds, news = refs[:4], refs[4:12], refs[12:]
        one, two, three, four = [ref[...].astype(jnp.float32) for ref in parts]
        own, other = one + two, three + four
        mine = bit_ref[0] == 0
        low, high = jnp.where(mine, own, other), jnp.where(mine, other, own)
        left = lax.broadcasted_iota(jnp.int32, (row_count, width), 1) < width // 2
        low_pair, high_pair = low[:, half:], high[:, half:]
        grads = (
            (0, (slice(None), slice(0, half)), low[:, :half]),
            (0, (slice(None), slice(half, columns)), high[:, :half]),
            (4, (slice(None), 0), jnp.where(left, low_pair, pltpu.roll(high_pair, width // 2, 1))),
            (4, (slice(None), 1), jnp.where(left, pltpu.roll(low_pair, width // 2, 1), high_pair)),
        )
        for first, where, grad in grads:
            results = adamw(
                grad,
                *[ref[where] for ref in olds[first : first + 4]],
                MATRIX_RATE,
                WEIGHT_DECAY,
                EMA_KEEP,
            )
            for ref, result in zip(news[first : first + 4], results):
                ref[where] = result

    outs = [jax.ShapeDtypeStruct(old.shape, jnp.float32) for old in queries + keyvals]
    results = pl.pallas_call(
        kernel,
        in_specs=[pl.BlockSpec(memory_space=pltpu.SMEM)]
        + [pl.BlockSpec(memory_space=pltpu.VMEM)] * 12,
        out_specs=[pl.BlockSpec(memory_space=pltpu.VMEM)] * 8,
        out_shape=outs,
        compiler_params=pltpu.CompilerParams(vmem_limit_bytes=32 * 2**20),
    )(pair_bit.reshape(1), *parts, *queries, *keyvals)
    return results[:4], results[4:]


def expand_update(parts, olds):
    row_count, planes, columns = olds[0].shape
    half = columns // 2
    chunks = chunks_of(half)
    step = 16

    def kernel(*refs):
        part_refs, old_refs, new_refs = refs[:2], refs[2:6], refs[6:]
        for (start, width), part_ref in zip(chunks, part_refs):
            for plane in range(planes):
                at = pl.ds(plane * width, width)
                for side in range(2):
                    where = (slice(None), plane, pl.ds(side * half + start, width))
                    results = adamw(
                        part_ref[side, :, at].astype(jnp.float32)
                        + part_ref[side + 2, :, at].astype(jnp.float32),
                        *[ref[where] for ref in old_refs],
                        MATRIX_RATE,
                        WEIGHT_DECAY,
                        EMA_KEEP,
                    )
                    for ref, result in zip(new_refs, results):
                        ref[where] = result

    def state_spec():
        return pl.BlockSpec((step, planes, columns), lambda i: (i, 0, 0))

    out = jax.ShapeDtypeStruct(olds[0].shape, jnp.float32)
    return pl.pallas_call(
        kernel,
        grid=(row_count // step,),
        in_specs=[
            pl.BlockSpec((4, step, planes * width), lambda i: (0, i, 0)) for _, width in chunks
        ]
        + [state_spec() for _ in range(4)],
        out_specs=[state_spec() for _ in range(4)],
        out_shape=(out,) * 4,
        compiler_params=pltpu.CompilerParams(vmem_limit_bytes=48 * 2**20),
    )(*parts, *olds)


def per_device(
    layer_input,
    upstream,
    doc_lengths,
    token_valid,
    query_weight,
    query_moment,
    query_second,
    query_shadow,
    keyval_weight,
    keyval_moment,
    keyval_second,
    keyval_shadow,
    mixing_weight,
    mixing_moment,
    mixing_second,
    mixing_shadow,
    expand_weight,
    expand_moment,
    expand_second,
    expand_shadow,
    contract_weight,
    contract_moment,
    contract_second,
    contract_shadow,
    norms_weight,
    norms_moment,
    norms_second,
    norms_shadow,
):
    bf_type = jnp.bfloat16
    fl_type = jnp.float32
    dp_count = lax.axis_size("dp")
    low_count = dp_count // 4
    dp_index = lax.axis_index("dp")
    outer_bit = dp_index // (2 * low_count)
    pair_bit = (dp_index // low_count) % 2
    low_index = dp_index % low_count
    core_bit = lax.axis_index("tensor")
    low_groups = [[base * low_count + low for low in range(low_count)] for base in range(4)]

    def move(value, target):
        return lax.ppermute(
            value,
            "dp",
            [
                (place * low_count + low, goal * low_count + low)
                for place, goal in target.items()
                for low in range(low_count)
            ],
        )

    place_groups = [
        [place * low_count + low for place in range(4)] for low in range(low_count)
    ]

    def spread(blocks):
        return lax.all_to_all(
            blocks, "dp", split_axis=0, concat_axis=0, tiled=True, axis_index_groups=place_groups
        )

    def swap(value, flip):
        return move(value, {place: place ^ flip for place in range(4)})

    def swap_low(value, flip):
        return lax.ppermute(value, "dp", [(index, index ^ flip) for index in range(dp_count)])

    def swap_pair(value):
        return swap(value, 1)

    def swap_core(value):
        return lax.ppermute(value, "tensor", [(0, 1), (1, 0)])

    def after(value, *earlier):
        return lax.optimization_barrier((value,) + earlier)[0]

    def pick(bit, zero, one):
        return jnp.where(bit == 0, zero, one)

    def gather_low(blocks):
        return lax.all_gather(blocks, "dp", axis=1, tiled=True, axis_index_groups=low_groups)

    def scatter_low(blocks):
        return lax.psum_scatter(
            blocks, "dp", scatter_dimension=1, tiled=True, axis_index_groups=low_groups
        )

    own_rows, model_width = query_weight.shape[0], norms_weight.shape[1] * dp_count * 2

    def exchange_columns(keep, send):
        return keep, swap(send, 1), swap(keep, 2), swap(send, 3)

    def join_columns(keep, one, two, three):
        low_pair = [pick(pair_bit, keep, one), pick(pair_bit, one, keep)]
        high_pair = [pick(pair_bit, two, three), pick(pair_bit, three, two)]
        return pick(outer_bit, jnp.stack(low_pair + high_pair), jnp.stack(high_pair + low_pair))

    def exchange_owned(rows):
        return rows, move(rows, {0: 2, 1: 0, 2: 3, 3: 1}), move(rows, {1: 2, 2: 1})

    def join_owned(rows, first, second):
        second = pick(outer_bit ^ pair_bit, rows, second)
        return pick(outer_bit, jnp.stack([second, first]), jnp.stack([first, second]))

    def flat(blocks):
        return blocks.reshape(-1, blocks.shape[-1])

    def exchange_low(blocks):
        return [blocks] + [swap_low(blocks, flip) for flip in range(1, low_count)]

    def gather_direct(moved):
        return flat(join_low(moved, low_index))

    def low_blocks(full, parts):
        blocks = full.reshape(parts, low_count, -1, full.shape[1])
        return [
            lax.dynamic_index_in_dim(blocks, low_index ^ flip, 1, keepdims=False)
            for flip in range(low_count)
        ]

    def sent_low(blocks):
        return [swap_low(block, flip) if flip else block for flip, block in enumerate(blocks)]

    def total_low(terms):
        return sum(term.astype(fl_type) for term in terms).astype(bf_type)

    def columns_moved(reduced):
        place = 2 * outer_bit + pair_bit
        kept, one, two, three = [
            lax.dynamic_index_in_dim(reduced, place ^ flip, 0, keepdims=False) for flip in range(4)
        ]
        return kept, swap(two, 2), swap(one, 1), swap(three, 3)

    def gather_tokens(rows):
        away = swap_pair(rows)
        return jnp.concatenate([rows, swap_core(rows), away, swap_core(away)])

    def token_sums(partial, hold=()):
        own, across, away, far = jnp.split(partial, 4)

        def over_cores(mine, sent):
            return mine + swap_core(sent.astype(bf_type)).astype(fl_type)

        return over_cores(own, across), after(over_cores(away, far).astype(bf_type), *hold)

    def scatter_tokens(partial, fill=lambda: (), hold=()):
        kept, sent = token_sums(partial, hold)
        return kept + after(swap_pair(sent), *fill()).astype(fl_type)

    group_len = token_valid.shape[1]
    doc_count = doc_lengths.shape[1]
    gain_count = norms_weight.size
    first_rows, last_blocks = cast_chunks(expand_weight, pair_bit)
    first_moved = exchange_columns(*first_rows)
    mixing_moved = exchange_owned(after(mixing_weight, first_rows[0]).astype(bf_type))
    own_facts = jnp.concatenate(
        [
            norms_weight.reshape(-1),
            doc_lengths[0].astype(fl_type),
            token_valid[0].astype(fl_type),
        ]
    )
    facts = lax.all_to_all(
        jnp.broadcast_to(
            own_facts[None], (2 * dp_count, own_facts.size)
        ),
        ("dp", "tensor"),
        split_axis=0,
        concat_axis=0,
        tiled=True,
    )
    gain_rows = facts[:, :gain_count].reshape(2 * dp_count, 2, -1).transpose(1, 0, 2)
    gain_rows = gain_rows.reshape(2, model_width)
    partner = 2 * (dp_index ^ low_count) + core_bit
    partner_facts = lax.dynamic_index_in_dim(facts, partner, 0, keepdims=False)[gain_count:]
    partner_facts = partner_facts.astype(jnp.int32)
    other_lengths, other_valid = partner_facts[:doc_count], partner_facts[doc_count:]
    input_rows = layer_input.astype(fl_type)
    normed = normalize(input_rows, gain_rows[0]).astype(bf_type)
    normed_all = gather_tokens(normed)
    qkv_quad = spread(after(cast_projections(query_weight, keyval_weight), normed))
    qkv_moved = exchange_low(after(qkv_quad, normed))
    first_low = flat(gather_low(join_columns(*after(first_moved, normed))))
    mixing_both = join_owned(*mixing_moved)
    last_quad = spread(after(last_blocks, mixing_both, qkv_quad))
    contract_moved = exchange_owned(after(contract_weight, last_quad).astype(bf_type))
    qkv_low = gather_direct(after(qkv_moved, mixing_both))
    mixing_low = gather_direct(exchange_low(after(mixing_both, qkv_low)))
    last_low = flat(gather_low(after(last_quad, normed_all)))
    contract_both = join_owned(*contract_moved)
    contract_low = flat(gather_low(contract_both))
    out_grad_all = gather_tokens(after(upstream, normed_all))
    places = (
        jnp.arange(group_len, dtype=jnp.int32) + core_bit * (group_len // 2)
    ) % group_len

    def ordered_valid(valid):
        first, second = valid[: group_len // 2], valid[group_len // 2 :]
        return pick(
            core_bit, jnp.concatenate([first, second]), jnp.concatenate([second, first])
        )

    position_one, allowed_one = layout(doc_lengths[0], ordered_valid(token_valid[0]), places)
    position_two, allowed_two = layout(other_lengths, ordered_valid(other_valid), places)
    allowed = (allowed_one, allowed_two)
    cosine_table, sine_table = rope_tables(
        jnp.concatenate([position_one, position_two]), HEAD_DIM
    )
    token_count = 2 * group_len
    query_width = query_weight.shape[1] // 2
    key_width = keyval_weight.shape[2] // 2
    head_count = query_width // HEAD_DIM
    kv_count = key_width // HEAD_DIM
    group_ratio = head_count // kv_count
    hidden_width = expand_weight.shape[2] // 2
    factor = HEAD_DIM ** (-0.5)
    qkv_pre = jnp.dot(normed_all, qkv_low, preferred_element_type=fl_type)
    queries = rotate(
        qkv_pre[:, :query_width].reshape(token_count, head_count, HEAD_DIM),
        cosine_table,
        sine_table,
    ).astype(bf_type)
    keys = rotate(
        qkv_pre[:, query_width : query_width + key_width].reshape(token_count, kv_count, HEAD_DIM),
        cosine_table,
        sine_table,
    ).astype(bf_type)
    values = (
        qkv_pre[:, query_width + key_width :]
        .reshape(token_count, kv_count, HEAD_DIM)
        .astype(bf_type)
    )


    def part(array, group_index, kv_index, heads):
        return array[
            group_index * group_len : (group_index + 1) * group_len,
            kv_index * heads : (kv_index + 1) * heads,
        ]

    def head_scores(group_index, kv_index):
        query_block = part(queries, group_index, kv_index, group_ratio)
        key_block = part(keys, group_index, kv_index, 1)[:, 0]
        raw_scores = (
            jnp.einsum("gre,ke->rgk", query_block, key_block, preferred_element_type=fl_type)
            * factor
        )
        return (query_block, key_block, jnp.where(allowed[group_index][None], raw_scores, NEG_FILL))

    mixed_groups = []
    log_totals = {}
    for group_index in range(2):
        mixed_parts = []
        for kv_index in range(kv_count):
            _, _, masked = head_scores(group_index, kv_index)
            largest = jnp.max(masked, axis=-1, keepdims=True)
            exp_scores = jnp.exp(masked - largest)
            totals = jnp.sum(exp_scores, axis=-1, keepdims=True)
            soft_probs = (exp_scores / totals).astype(bf_type)
            log_totals[group_index, kv_index] = largest + jnp.log(totals)
            mixed_parts.append(
                jnp.einsum(
                    "rgk,ke->gre",
                    soft_probs,
                    part(values, group_index, kv_index, 1)[:, 0],
                    preferred_element_type=fl_type,
                )
            )
        mixed_groups.append(jnp.concatenate(mixed_parts, axis=1))
    mixed = jnp.concatenate(mixed_groups).reshape(token_count, query_width).astype(bf_type)
    attended = scatter_tokens(
        jnp.dot(after(mixed, out_grad_all), mixing_low, preferred_element_type=fl_type),
        lambda: (contract_both,),
    )
    middle = input_rows + attended
    normed_two = normalize(middle, gain_rows[1]).astype(bf_type)
    normed_two_all = gather_tokens(normed_two)
    def gated(rows, weights):
        gate_up = jnp.dot(rows, weights, preferred_element_type=fl_type)
        return jnp.split(gate_up, 2, axis=1)

    gate_first, up_first = gated(normed_two_all, first_low)
    gate_last, up_last = gated(after(normed_two_all, gate_first), last_low)
    hidden = jnp.concatenate(
        [
            (jax.nn.silu(gate) * up).astype(bf_type)
            for gate, up in ((gate_first, up_first), (gate_last, up_last))
        ],
        axis=1,
    )
    out_grad = upstream.astype(fl_type)

    def reduce_columns(full):
        return scatter_low(full.reshape(4, low_count * own_rows, full.shape[1]))

    def reduce_owned(full):
        return scatter_low(full.reshape(2, full.shape[0] // 2, full.shape[1]))

    def owned_sent(reduced):
        rest = pick(outer_bit, reduced[0], reduced[1])
        first = move(pick(outer_bit, reduced[1], reduced[0]), {0: 1, 1: 3, 2: 0, 3: 2})
        return first, rest, move(rest, {1: 2, 2: 1})

    def owned_total(first, rest, second):
        return first.astype(fl_type) + pick(outer_bit ^ pair_bit, rest, second).astype(fl_type)

    contract_full = lax.dot_general(
        hidden, out_grad_all, CONTRACT_FIRST, preferred_element_type=fl_type
    ).astype(bf_type)
    contract_reduced = reduce_owned(contract_full)
    hidden_grad = lax.dot_general(
        after(out_grad_all, contract_full), contract_low, CONTRACT_LAST, preferred_element_type=fl_type
    )

    def gated_grad(gate, up, grad):
        gate_sig = jax.nn.sigmoid(gate)
        gate_grad = grad * up * gate_sig * (1.0 + gate * (1.0 - gate_sig))
        up_grad = grad * (gate * gate_sig)
        return jnp.concatenate([gate_grad.astype(bf_type), up_grad.astype(bf_type)], axis=1)

    first_width = first_low.shape[1] // 2
    first_grad = gated_grad(gate_first, up_first, hidden_grad[:, :first_width])
    last_grad = gated_grad(gate_last, up_last, hidden_grad[:, first_width:])
    last_full = lax.dot_general(
        normed_two_all, last_grad, CONTRACT_FIRST, preferred_element_type=fl_type
    ).astype(bf_type)
    first_full = lax.dot_general(
        after(normed_two_all, last_full),
        first_grad,
        CONTRACT_FIRST,
        preferred_element_type=fl_type,
    ).astype(bf_type)
    last_reduced, first_reduced = reduce_columns(last_full), reduce_columns(first_full)
    normed_two_partial = lax.dot_general(
        after(last_grad, first_full), last_low, CONTRACT_LAST, preferred_element_type=fl_type
    ) + lax.dot_general(first_grad, first_low, CONTRACT_LAST, preferred_element_type=fl_type)
    branch_partial = jnp.dot(
        after(hidden, normed_two_partial), contract_low, preferred_element_type=fl_type
    )
    normed_two_grad = scatter_tokens(normed_two_partial, lambda: (branch_partial,))
    middle_pull = jax.vjp(normalize, middle, gain_rows[1])[1]
    middle_part, gain_two_grad = middle_pull(normed_two_grad)
    middle_grad = out_grad + middle_part
    attended_all = gather_tokens(middle_grad.astype(bf_type))
    contract_sent = owned_sent(after(contract_reduced, middle_grad))
    mixing_full = lax.dot_general(
        mixed, attended_all, CONTRACT_FIRST, preferred_element_type=fl_type
    ).astype(bf_type)
    mixing_reduced = reduce_owned(mixing_full)
    attended_all = after(attended_all, mixing_full)
    mixed_grad = (
        lax.dot_general(attended_all, mixing_low, CONTRACT_LAST, preferred_element_type=fl_type)
        .astype(bf_type)
        .reshape(token_count, head_count, HEAD_DIM)
    )
    mixed_grad = after(mixed_grad, last_reduced)
    last_parts = spread(last_reduced)
    query_grads = []
    key_grads = []
    value_grads = []
    for group_index in range(2):
        if group_index == 1:
            mixed_grad = after(mixed_grad, query_grads[0], *contract_sent)
        for kv_index in range(kv_count):
            query_block, key_block, masked = head_scores(group_index, kv_index)
            soft_exact = jnp.exp(masked - log_totals[group_index, kv_index])
            out_block = part(mixed_grad, group_index, kv_index, group_ratio)
            prob_grad = jnp.einsum(
                "gre,ke->rgk",
                out_block,
                part(values, group_index, kv_index, 1)[:, 0],
                preferred_element_type=fl_type,
            )
            inner_sum = jnp.sum(prob_grad * soft_exact, axis=-1, keepdims=True)
            score_grad = (soft_exact * (prob_grad - inner_sum)).astype(bf_type)
            if group_index == 1:
                score_grad = after(score_grad, last_parts)
            query_grads.append(
                jnp.einsum("rgk,ke->gre", score_grad, key_block, preferred_element_type=fl_type)
                * factor
            )
            key_grads.append(
                jnp.einsum("rgk,gre->ke", score_grad, query_block, preferred_element_type=fl_type)
                * factor
            )
            value_grads.append(
                jnp.einsum(
                    "rgk,gre->ke",
                    soft_exact.astype(bf_type),
                    out_block,
                    preferred_element_type=fl_type,
                )
            )

    def assemble(blocks, axis):
        return jnp.concatenate(
            [
                jnp.concatenate(blocks[:kv_count], axis=axis),
                jnp.concatenate(blocks[kv_count:], axis=axis),
            ]
        )

    query_back = (
        rotate(assemble(query_grads, 1), cosine_table, -sine_table)
        .astype(bf_type)
        .reshape(token_count, query_width)
    )
    key_back = rotate(
        assemble(key_grads, 1).reshape(token_count, kv_count, HEAD_DIM), cosine_table, -sine_table
    ).reshape(token_count, key_width)
    value_back = assemble(value_grads, 1)
    qkv_back = jnp.concatenate(
        [query_back, key_back.astype(bf_type), value_back.astype(bf_type)], axis=1
    )
    expand_states = [expand_weight, expand_moment, expand_second, expand_shadow]
    branch = scatter_tokens(
        branch_partial, lambda: (query_grads[-1],), hold=(attended_all,)
    )
    layer_output = (middle + branch).astype(bf_type)
    contract_news = adamw(
        owned_total(*contract_sent),
        contract_weight,
        contract_moment,
        contract_second,
        contract_shadow,
        MATRIX_RATE,
        WEIGHT_DECAY,
        EMA_KEEP,
    )
    qkv_back = after(qkv_back, layer_output, last_parts)
    qkv_full = lax.dot_general(
        normed_all, qkv_back, CONTRACT_FIRST, preferred_element_type=fl_type
    ).astype(bf_type)
    qkv_blocks = low_blocks(qkv_full, 4)
    qkv_moved = sent_low(qkv_blocks)
    normed_partial = lax.dot_general(
        after(qkv_back, *qkv_blocks), qkv_low, CONTRACT_LAST, preferred_element_type=fl_type
    )
    first_parts = spread(after(first_reduced, normed_partial))
    normed_kept, normed_sent = token_sums(normed_partial)
    normed_away = swap_pair(normed_sent)
    qkv_total = total_low(after(qkv_moved, normed_sent))
    normed_away = after(normed_away, first_parts, qkv_total, *contract_news)
    normed_grad = normed_kept + normed_away.astype(fl_type)
    expand_news = expand_update((first_parts, last_parts), expand_states)
    qkv_parts = after(columns_moved(qkv_total), *expand_news)
    mixing_grad = owned_total(*owned_sent(after(mixing_reduced, first_parts)))
    rows_pull = jax.vjp(normalize, input_rows, gain_rows[0])[1]
    rows_part, gain_one_grad = rows_pull(normed_grad)
    input_grad = middle_grad + rows_part
    gain_parts = after(jnp.stack([gain_one_grad, gain_two_grad]), first_parts).reshape(2, 2 * dp_count, -1)
    gain_sums = jnp.sum(
        lax.all_to_all(gain_parts, ("dp", "tensor"), split_axis=1, concat_axis=1, tiled=True),
        axis=1,
    )
    (
        (query_master, query_momentum, query_variance, query_average),
        (keyval_master, keyval_momentum, keyval_variance, keyval_average),
    ) = projection_update(
        qkv_parts,
        pair_bit,
        [query_weight, query_moment, query_second, query_shadow],
        [keyval_weight, keyval_moment, keyval_second, keyval_shadow],
    )
    mixing_master, mixing_momentum, mixing_variance, mixing_average = adamw(
        mixing_grad,
        mixing_weight,
        mixing_moment,
        mixing_second,
        mixing_shadow,
        MATRIX_RATE,
        WEIGHT_DECAY,
        EMA_KEEP,
    )
    expand_master, expand_momentum, expand_variance, expand_average = expand_news
    contract_master, contract_momentum, contract_variance, contract_average = contract_news
    norms_master, norms_momentum, norms_variance, norms_average = adamw(
        gain_sums, norms_weight, norms_moment, norms_second, norms_shadow, GAIN_RATE, 0.0, GAIN_KEEP
    )
    return (
        layer_output,
        input_grad,
        query_master,
        query_momentum,
        query_variance,
        query_average,
        keyval_master,
        keyval_momentum,
        keyval_variance,
        keyval_average,
        mixing_master,
        mixing_momentum,
        mixing_variance,
        mixing_average,
        expand_master,
        expand_momentum,
        expand_variance,
        expand_average,
        contract_master,
        contract_momentum,
        contract_variance,
        contract_average,
        norms_master,
        norms_momentum,
        norms_variance,
        norms_average,
    )


def solution(mesh):
    in_specs = (
        P(("dp", "tensor"), None),
        P(("dp", "tensor"), None),
        P("dp", None),
        P("dp", None),
        P("dp", "tensor"),
        P("dp", "tensor"),
        P("dp", "tensor"),
        P("dp", "tensor"),
        P("dp", None, "tensor"),
        P("dp", None, "tensor"),
        P("dp", None, "tensor"),
        P("dp", None, "tensor"),
        P(("tensor", "dp"), None),
        P(("tensor", "dp"), None),
        P(("tensor", "dp"), None),
        P(("tensor", "dp"), None),
        P("dp", None, "tensor"),
        P("dp", None, "tensor"),
        P("dp", None, "tensor"),
        P("dp", None, "tensor"),
        P(("tensor", "dp"), None),
        P(("tensor", "dp"), None),
        P(("tensor", "dp"), None),
        P(("tensor", "dp"), None),
        P(None, ("dp", "tensor")),
        P(None, ("dp", "tensor")),
        P(None, ("dp", "tensor")),
        P(None, ("dp", "tensor")),
    )
    out_specs = (
        P(("dp", "tensor"), None),
        P(("dp", "tensor"), None),
        P("dp", "tensor"),
        P("dp", "tensor"),
        P("dp", "tensor"),
        P("dp", "tensor"),
        P("dp", None, "tensor"),
        P("dp", None, "tensor"),
        P("dp", None, "tensor"),
        P("dp", None, "tensor"),
        P(("tensor", "dp"), None),
        P(("tensor", "dp"), None),
        P(("tensor", "dp"), None),
        P(("tensor", "dp"), None),
        P("dp", None, "tensor"),
        P("dp", None, "tensor"),
        P("dp", None, "tensor"),
        P("dp", None, "tensor"),
        P(("tensor", "dp"), None),
        P(("tensor", "dp"), None),
        P(("tensor", "dp"), None),
        P(("tensor", "dp"), None),
        P(None, ("dp", "tensor")),
        P(None, ("dp", "tensor")),
        P(None, ("dp", "tensor")),
        P(None, ("dp", "tensor")),
    )
    return jax.shard_map(
        per_device, mesh=mesh, in_specs=in_specs, out_specs=out_specs, check_vma=False
    )
```

```python
import jax
import jax.numpy as jnp
from jax import lax
from jax.experimental import pallas as pl
from jax.experimental.pallas import tpu as pltpu
from jax.sharding import PartitionSpec as P

HEAD_DIM = 64
STEP = 5


NORM_EPS = 1e-05
NEG_FILL = -1e30
ROPE_BASE = 10000.0
BETA_ONE = 0.5
BETA_TWO = 0.5
ADAM_EPS = 1e-08
WEIGHT_DECAY = 0.1
MATRIX_RATE = 0.02
GAIN_RATE = 0.2
EMA_KEEP = 0.9
GAIN_KEEP = 0.5
CONTRACT_LAST = (((1,), (1,)), ((), ()))
CONTRACT_FIRST = (((0,), (0,)), ((), ()))


def normalize(field_rows, gain_row):
    factor = lax.rsqrt(jnp.mean(field_rows * field_rows, axis=-1, keepdims=True) + NORM_EPS)
    return field_rows * factor * gain_row


def rotate(field, cosine_table, sine_table):
    half_dim = field.shape[-1] // 2
    first_half = field[..., :half_dim]
    second_half = field[..., half_dim:]
    return jnp.concatenate(
        [
            first_half * cosine_table - second_half * sine_table,
            second_half * cosine_table + first_half * sine_table,
        ],
        axis=-1,
    )


def layout(lengths, valid_keys, places):
    doc_ends = jnp.cumsum(lengths)
    doc_starts = doc_ends - lengths
    segment = jnp.sum((doc_ends[None, :] <= places[:, None]).astype(jnp.int32), axis=1)
    owned_doc = segment[:, None] == jnp.arange(lengths.shape[0], dtype=jnp.int32)[None, :]
    position = places - jnp.sum(jnp.where(owned_doc, doc_starts[None, :], 0), axis=1)
    allowed = (
        (segment[:, None] == segment[None, :])
        & (places[None, :] <= places[:, None])
        & ((valid_keys[None, :] == 1) | (places[:, None] == places[None, :]))
    )
    return (position, allowed)


def rope_tables(position, head_size):
    half_dim = head_size // 2
    inverse = ROPE_BASE ** (-(2.0 * jnp.arange(half_dim, dtype=jnp.float32)) / head_size)
    angles = position.astype(jnp.float32)[:, None] * inverse[None, :]
    return (jnp.cos(angles)[:, None, :], jnp.sin(angles)[:, None, :])


def adamw(grad_value, weight, moment, second, shadow, step_rate, decay_rate, keep_rate):
    moment_new = BETA_ONE * moment + (1.0 - BETA_ONE) * grad_value
    second_new = BETA_TWO * second + (1.0 - BETA_TWO) * grad_value * grad_value
    moment_hat = moment_new / (1.0 - BETA_ONE**STEP)
    second_hat = second_new / (1.0 - BETA_TWO**STEP)
    weight_new = weight - step_rate * (
        moment_hat / (jnp.sqrt(second_hat) + ADAM_EPS) + decay_rate * weight
    )
    shadow_new = keep_rate * shadow + (1.0 - keep_rate) * weight_new
    return (weight_new, moment_new, second_new, shadow_new)


def chunks_of(width):
    first = width // 256 * 128
    return ((0, first), (first, width - first))


def cast_chunks(weight, pair_bit):
    row_count, planes, columns = weight.shape
    half = columns // 2
    chunks = chunks_of(half)

    def kernel(bit_ref, weight_ref, keep_ref, send_ref, last_ref):
        mine = bit_ref[0] == 0
        for number, (start, width) in enumerate(chunks):
            for plane in range(planes):
                low, high = [
                    weight_ref[:, plane, pl.ds(side * half + start, width)].astype(jnp.bfloat16)
                    for side in range(2)
                ]
                at = pl.ds(plane * width, width)
                if number == 0:
                    keep_ref[:, at] = jnp.where(mine, low, high)
                    send_ref[:, at] = jnp.where(mine, high, low)
                else:
                    for outer in range(2):
                        last_ref[2 * outer, :, at] = low
                        last_ref[2 * outer + 1, :, at] = high

    first, last = [planes * width for _, width in chunks]
    step = 32
    rows = pl.BlockSpec((step, first), lambda i, bit: (i, 0))
    keep, send, blocks = pl.pallas_call(
        kernel,
        grid_spec=pltpu.PrefetchScalarGridSpec(
            num_scalar_prefetch=1,
            grid=(row_count // step,),
            in_specs=[pl.BlockSpec((step, planes, columns), lambda i, bit: (i, 0, 0))],
            out_specs=[rows, rows, pl.BlockSpec((4, step, last), lambda i, bit: (0, i, 0))],
        ),
        out_shape=[
            jax.ShapeDtypeStruct((row_count, first), jnp.bfloat16),
            jax.ShapeDtypeStruct((row_count, first), jnp.bfloat16),
            jax.ShapeDtypeStruct((4, row_count, last), jnp.bfloat16),
        ],
        compiler_params=pltpu.CompilerParams(vmem_limit_bytes=32 * 2**20),
    )(pair_bit.reshape(1), weight)
    return (keep, send), blocks


def join_low(blocks, low_index):
    parts, rows, columns = blocks[0].shape
    count = len(blocks)

    def kernel(low_ref, *refs):
        for flip in range(count):
            refs[count][0, low_ref[0] ^ flip] = refs[flip][0]

    return pl.pallas_call(
        kernel,
        grid_spec=pltpu.PrefetchScalarGridSpec(
            num_scalar_prefetch=1,
            grid=(parts,),
            in_specs=[pl.BlockSpec((1, rows, columns), lambda i, low: (i, 0, 0))] * count,
            out_specs=pl.BlockSpec((1, count, rows, columns), lambda i, low: (i, 0, 0, 0)),
        ),
        out_shape=jax.ShapeDtypeStruct((parts, count, rows, columns), blocks[0].dtype),
        compiler_params=pltpu.CompilerParams(vmem_limit_bytes=32 * 2**20),
    )(low_index.reshape(1), *blocks)


def cast_projections(query, keyval):
    row_count, columns = query.shape
    half, width = columns // 2, keyval.shape[2]

    def kernel(query_ref, keyval_ref, out_ref):
        left = lax.broadcasted_iota(jnp.int32, (row_count, width), 1) < width // 2
        key, value = keyval_ref[:, 0, :], keyval_ref[:, 1, :]
        pairs = (
            jnp.where(left, key, pltpu.roll(value, width // 2, 1)).astype(jnp.bfloat16),
            jnp.where(left, pltpu.roll(key, width // 2, 1), value).astype(jnp.bfloat16),
        )
        for place in range(4):
            side = place % 2
            part = query_ref[:, pl.ds(side * half, half)]
            out_ref[place, :, :half] = part.astype(jnp.bfloat16)
            out_ref[place, :, half:] = pairs[side]

    return pl.pallas_call(
        kernel,
        in_specs=[pl.BlockSpec(memory_space=pltpu.VMEM)] * 2,
        out_specs=pl.BlockSpec(memory_space=pltpu.VMEM),
        out_shape=jax.ShapeDtypeStruct((4, row_count, half + width), jnp.bfloat16),
        compiler_params=pltpu.CompilerParams(vmem_limit_bytes=16 * 2**20),
    )(query, keyval)


def projection_update(parts, pair_bit, queries, keyvals):
    row_count, columns = queries[0].shape
    half, width = columns // 2, keyvals[0].shape[2]

    def kernel(bit_ref, *refs):
        parts, olds, news = refs[:4], refs[4:12], refs[12:]
        one, two, three, four = [ref[...].astype(jnp.float32) for ref in parts]
        own, other = one + two, three + four
        mine = bit_ref[0] == 0
        low, high = jnp.where(mine, own, other), jnp.where(mine, other, own)
        left = lax.broadcasted_iota(jnp.int32, (row_count, width), 1) < width // 2
        low_pair, high_pair = low[:, half:], high[:, half:]
        grads = (
            (0, (slice(None), slice(0, half)), low[:, :half]),
            (0, (slice(None), slice(half, columns)), high[:, :half]),
            (4, (slice(None), 0), jnp.where(left, low_pair, pltpu.roll(high_pair, width // 2, 1))),
            (4, (slice(None), 1), jnp.where(left, pltpu.roll(low_pair, width // 2, 1), high_pair)),
        )
        for first, where, grad in grads:
            results = adamw(
                grad,
                *[ref[where] for ref in olds[first : first + 4]],
                MATRIX_RATE,
                WEIGHT_DECAY,
                EMA_KEEP,
            )
            for ref, result in zip(news[first : first + 4], results):
                ref[where] = result

    outs = [jax.ShapeDtypeStruct(old.shape, jnp.float32) for old in queries + keyvals]
    results = pl.pallas_call(
        kernel,
        in_specs=[pl.BlockSpec(memory_space=pltpu.SMEM)]
        + [pl.BlockSpec(memory_space=pltpu.VMEM)] * 12,
        out_specs=[pl.BlockSpec(memory_space=pltpu.VMEM)] * 8,
        out_shape=outs,
        compiler_params=pltpu.CompilerParams(vmem_limit_bytes=32 * 2**20),
    )(pair_bit.reshape(1), *parts, *queries, *keyvals)
    return results[:4], results[4:]


def expand_update(parts, olds):
    row_count, planes, columns = olds[0].shape
    half = columns // 2
    chunks = chunks_of(half)
    step = 16

    def kernel(*refs):
        part_refs, old_refs, new_refs = refs[:2], refs[2:6], refs[6:]
        for (start, width), part_ref in zip(chunks, part_refs):
            for plane in range(planes):
                at = pl.ds(plane * width, width)
                for side in range(2):
                    where = (slice(None), plane, pl.ds(side * half + start, width))
                    results = adamw(
                        part_ref[side, :, at].astype(jnp.float32)
                        + part_ref[side + 2, :, at].astype(jnp.float32),
                        *[ref[where] for ref in old_refs],
                        MATRIX_RATE,
                        WEIGHT_DECAY,
                        EMA_KEEP,
                    )
                    for ref, result in zip(new_refs, results):
                        ref[where] = result

    def state_spec():
        return pl.BlockSpec((step, planes, columns), lambda i: (i, 0, 0))

    out = jax.ShapeDtypeStruct(olds[0].shape, jnp.float32)
    return pl.pallas_call(
        kernel,
        grid=(row_count // step,),
        in_specs=[
            pl.BlockSpec((4, step, planes * width), lambda i: (0, i, 0)) for _, width in chunks
        ]
        + [state_spec() for _ in range(4)],
        out_specs=[state_spec() for _ in range(4)],
        out_shape=(out,) * 4,
        compiler_params=pltpu.CompilerParams(vmem_limit_bytes=48 * 2**20),
    )(*parts, *olds)


def per_device(
    layer_input,
    upstream,
    doc_lengths,
    token_valid,
    query_weight,
    query_moment,
    query_second,
    query_shadow,
    keyval_weight,
    keyval_moment,
    keyval_second,
    keyval_shadow,
    mixing_weight,
    mixing_moment,
    mixing_second,
    mixing_shadow,
    expand_weight,
    expand_moment,
    expand_second,
    expand_shadow,
    contract_weight,
    contract_moment,
    contract_second,
    contract_shadow,
    norms_weight,
    norms_moment,
    norms_second,
    norms_shadow,
):
    bf_type = jnp.bfloat16
    fl_type = jnp.float32
    dp_count = lax.axis_size("dp")
    low_count = dp_count // 4
    dp_index = lax.axis_index("dp")
    outer_bit = dp_index // (2 * low_count)
    pair_bit = (dp_index // low_count) % 2
    low_index = dp_index % low_count
    core_bit = lax.axis_index("tensor")
    low_groups = [[base * low_count + low for low in range(low_count)] for base in range(4)]

    def move(value, target):
        return lax.ppermute(
            value,
            "dp",
            [
                (place * low_count + low, goal * low_count + low)
                for place, goal in target.items()
                for low in range(low_count)
            ],
        )

    place_groups = [
        [place * low_count + low for place in range(4)] for low in range(low_count)
    ]

    def spread(blocks):
        return lax.all_to_all(
            blocks, "dp", split_axis=0, concat_axis=0, tiled=True, axis_index_groups=place_groups
        )

    def swap(value, flip):
        return move(value, {place: place ^ flip for place in range(4)})

    def swap_low(value, flip):
        return lax.ppermute(value, "dp", [(index, index ^ flip) for index in range(dp_count)])

    def swap_pair(value):
        return swap(value, 1)

    def swap_core(value):
        return lax.ppermute(value, "tensor", [(0, 1), (1, 0)])

    def after(value, *earlier):
        return lax.optimization_barrier((value,) + earlier)[0]

    def pick(bit, zero, one):
        return jnp.where(bit == 0, zero, one)

    def gather_low(blocks):
        return lax.all_gather(blocks, "dp", axis=1, tiled=True, axis_index_groups=low_groups)

    def scatter_low(blocks):
        return lax.psum_scatter(
            blocks, "dp", scatter_dimension=1, tiled=True, axis_index_groups=low_groups
        )

    own_rows, model_width = query_weight.shape[0], norms_weight.shape[1] * dp_count * 2

    def exchange_columns(keep, send):
        return keep, swap(send, 1), swap(keep, 2), swap(send, 3)

    def join_columns(keep, one, two, three):
        low_pair = [pick(pair_bit, keep, one), pick(pair_bit, one, keep)]
        high_pair = [pick(pair_bit, two, three), pick(pair_bit, three, two)]
        return pick(outer_bit, jnp.stack(low_pair + high_pair), jnp.stack(high_pair + low_pair))

    def exchange_owned(rows):
        return rows, move(rows, {0: 2, 1: 0, 2: 3, 3: 1}), move(rows, {1: 2, 2: 1})

    def join_owned(rows, first, second):
        second = pick(outer_bit ^ pair_bit, rows, second)
        return pick(outer_bit, jnp.stack([second, first]), jnp.stack([first, second]))

    def flat(blocks):
        return blocks.reshape(-1, blocks.shape[-1])

    def exchange_low(blocks):
        return [blocks] + [swap_low(blocks, flip) for flip in range(1, low_count)]

    def gather_direct(moved):
        return flat(join_low(moved, low_index))

    def low_blocks(full, parts):
        blocks = full.reshape(parts, low_count, -1, full.shape[1])
        return [
            lax.dynamic_index_in_dim(blocks, low_index ^ flip, 1, keepdims=False)
            for flip in range(low_count)
        ]

    def sent_low(blocks):
        return [swap_low(block, flip) if flip else block for flip, block in enumerate(blocks)]

    def total_low(terms):
        return sum(term.astype(fl_type) for term in terms).astype(bf_type)

    def columns_moved(reduced):
        place = 2 * outer_bit + pair_bit
        kept, one, two, three = [
            lax.dynamic_index_in_dim(reduced, place ^ flip, 0, keepdims=False) for flip in range(4)
        ]
        return kept, swap(two, 2), swap(one, 1), swap(three, 3)

    def gather_tokens(rows):
        away = swap_pair(rows)
        return jnp.concatenate([rows, swap_core(rows), away, swap_core(away)])

    def token_sums(partial, hold=()):
        own, across, away, far = jnp.split(partial, 4)

        def over_cores(mine, sent):
            return mine + swap_core(sent.astype(bf_type)).astype(fl_type)

        return over_cores(own, across), after(over_cores(away, far).astype(bf_type), *hold)

    def scatter_tokens(partial, fill=lambda: (), hold=()):
        kept, sent = token_sums(partial, hold)
        return kept + after(swap_pair(sent), *fill()).astype(fl_type)

    group_len = token_valid.shape[1]
    doc_count = doc_lengths.shape[1]
    gain_count = norms_weight.size
    first_rows, last_blocks = cast_chunks(expand_weight, pair_bit)
    first_moved = exchange_columns(*first_rows)
    mixing_moved = exchange_owned(after(mixing_weight, first_rows[0]).astype(bf_type))
    own_facts = jnp.concatenate(
        [
            norms_weight.reshape(-1),
            doc_lengths[0].astype(fl_type),
            token_valid[0].astype(fl_type),
        ]
    )
    facts = lax.all_to_all(
        jnp.broadcast_to(
            own_facts[None], (2 * dp_count, own_facts.size)
        ),
        ("dp", "tensor"),
        split_axis=0,
        concat_axis=0,
        tiled=True,
    )
    gain_rows = facts[:, :gain_count].reshape(2 * dp_count, 2, -1).transpose(1, 0, 2)
    gain_rows = gain_rows.reshape(2, model_width)
    partner = 2 * (dp_index ^ low_count) + core_bit
    partner_facts = lax.dynamic_index_in_dim(facts, partner, 0, keepdims=False)[gain_count:]
    partner_facts = partner_facts.astype(jnp.int32)
    other_lengths, other_valid = partner_facts[:doc_count], partner_facts[doc_count:]
    input_rows = layer_input.astype(fl_type)
    normed = normalize(input_rows, gain_rows[0]).astype(bf_type)
    normed_all = gather_tokens(normed)
    qkv_quad = spread(after(cast_projections(query_weight, keyval_weight), normed))
    qkv_moved = exchange_low(after(qkv_quad, normed))
    first_low = flat(gather_low(join_columns(*after(first_moved, normed))))
    mixing_both = join_owned(*mixing_moved)
    last_quad = spread(after(last_blocks, mixing_both, qkv_quad))
    contract_moved = exchange_owned(after(contract_weight, last_quad).astype(bf_type))
    qkv_low = gather_direct(after(qkv_moved, mixing_both))
    mixing_low = gather_direct(exchange_low(after(mixing_both, qkv_low)))
    last_low = flat(gather_low(after(last_quad, normed_all)))
    contract_both = join_owned(*contract_moved)
    contract_low = flat(gather_low(contract_both))
    out_grad_all = gather_tokens(after(upstream, normed_all))
    places = (
        jnp.arange(group_len, dtype=jnp.int32) + core_bit * (group_len // 2)
    ) % group_len

    def ordered_valid(valid):
        first, second = valid[: group_len // 2], valid[group_len // 2 :]
        return pick(
            core_bit, jnp.concatenate([first, second]), jnp.concatenate([second, first])
        )

    position_one, allowed_one = layout(doc_lengths[0], ordered_valid(token_valid[0]), places)
    position_two, allowed_two = layout(other_lengths, ordered_valid(other_valid), places)
    allowed = (allowed_one, allowed_two)
    cosine_table, sine_table = rope_tables(
        jnp.concatenate([position_one, position_two]), HEAD_DIM
    )
    token_count = 2 * group_len
    query_width = query_weight.shape[1] // 2
    key_width = keyval_weight.shape[2] // 2
    head_count = query_width // HEAD_DIM
    kv_count = key_width // HEAD_DIM
    group_ratio = head_count // kv_count
    hidden_width = expand_weight.shape[2] // 2
    factor = HEAD_DIM ** (-0.5)
    qkv_pre = jnp.dot(normed_all, qkv_low, preferred_element_type=fl_type)
    queries = rotate(
        qkv_pre[:, :query_width].reshape(token_count, head_count, HEAD_DIM),
        cosine_table,
        sine_table,
    ).astype(bf_type)
    keys = rotate(
        qkv_pre[:, query_width : query_width + key_width].reshape(token_count, kv_count, HEAD_DIM),
        cosine_table,
        sine_table,
    ).astype(bf_type)
    values = (
        qkv_pre[:, query_width + key_width :]
        .reshape(token_count, kv_count, HEAD_DIM)
        .astype(bf_type)
    )


    def part(array, group_index, kv_index, heads):
        return array[
            group_index * group_len : (group_index + 1) * group_len,
            kv_index * heads : (kv_index + 1) * heads,
        ]

    def head_scores(group_index, kv_index):
        query_block = part(queries, group_index, kv_index, group_ratio)
        key_block = part(keys, group_index, kv_index, 1)[:, 0]
        raw_scores = (
            jnp.einsum("gre,ke->rgk", query_block, key_block, preferred_element_type=fl_type)
            * factor
        )
        return (query_block, key_block, jnp.where(allowed[group_index][None], raw_scores, NEG_FILL))

    mixed_groups = []
    log_totals = {}
    for group_index in range(2):
        mixed_parts = []
        for kv_index in range(kv_count):
            _, _, masked = head_scores(group_index, kv_index)
            largest = jnp.max(masked, axis=-1, keepdims=True)
            exp_scores = jnp.exp(masked - largest)
            totals = jnp.sum(exp_scores, axis=-1, keepdims=True)
            soft_probs = (exp_scores / totals).astype(bf_type)
            log_totals[group_index, kv_index] = largest + jnp.log(totals)
            mixed_parts.append(
                jnp.einsum(
                    "rgk,ke->gre",
                    soft_probs,
                    part(values, group_index, kv_index, 1)[:, 0],
                    preferred_element_type=fl_type,
                )
            )
        mixed_groups.append(jnp.concatenate(mixed_parts, axis=1))
    mixed = jnp.concatenate(mixed_groups).reshape(token_count, query_width).astype(bf_type)
    attended = scatter_tokens(
        jnp.dot(after(mixed, out_grad_all), mixing_low, preferred_element_type=fl_type),
        lambda: (contract_both,),
    )
    middle = input_rows + attended
    normed_two = normalize(middle, gain_rows[1]).astype(bf_type)
    normed_two_all = gather_tokens(normed_two)
    def gated(rows, weights):
        gate_up = jnp.dot(rows, weights, preferred_element_type=fl_type)
        return jnp.split(gate_up, 2, axis=1)

    gate_first, up_first = gated(normed_two_all, first_low)
    gate_last, up_last = gated(after(normed_two_all, gate_first), last_low)
    hidden = jnp.concatenate(
        [
            (jax.nn.silu(gate) * up).astype(bf_type)
            for gate, up in ((gate_first, up_first), (gate_last, up_last))
        ],
        axis=1,
    )
    out_grad = upstream.astype(fl_type)

    def reduce_columns(full):
        return scatter_low(full.reshape(4, low_count * own_rows, full.shape[1]))

    def reduce_owned(full):
        return scatter_low(full.reshape(2, full.shape[0] // 2, full.shape[1]))

    def owned_sent(reduced):
        rest = pick(outer_bit, reduced[0], reduced[1])
        first = move(pick(outer_bit, reduced[1], reduced[0]), {0: 1, 1: 3, 2: 0, 3: 2})
        return first, rest, move(rest, {1: 2, 2: 1})

    def owned_total(first, rest, second):
        return first.astype(fl_type) + pick(outer_bit ^ pair_bit, rest, second).astype(fl_type)

    contract_full = lax.dot_general(
        hidden, out_grad_all, CONTRACT_FIRST, preferred_element_type=fl_type
    ).astype(bf_type)
    contract_reduced = reduce_owned(contract_full)
    hidden_grad = lax.dot_general(
        after(out_grad_all, contract_full), contract_low, CONTRACT_LAST, preferred_element_type=fl_type
    )

    def gated_grad(gate, up, grad):
        gate_sig = jax.nn.sigmoid(gate)
        gate_grad = grad * up * gate_sig * (1.0 + gate * (1.0 - gate_sig))
        up_grad = grad * (gate * gate_sig)
        return jnp.concatenate([gate_grad.astype(bf_type), up_grad.astype(bf_type)], axis=1)

    first_width = first_low.shape[1] // 2
    first_grad = gated_grad(gate_first, up_first, hidden_grad[:, :first_width])
    last_grad = gated_grad(gate_last, up_last, hidden_grad[:, first_width:])
    last_full = lax.dot_general(
        normed_two_all, last_grad, CONTRACT_FIRST, preferred_element_type=fl_type
    ).astype(bf_type)
    first_full = lax.dot_general(
        after(normed_two_all, last_full),
        first_grad,
        CONTRACT_FIRST,
        preferred_element_type=fl_type,
    ).astype(bf_type)
    last_reduced, first_reduced = reduce_columns(last_full), reduce_columns(first_full)
    normed_two_partial = lax.dot_general(
        after(last_grad, first_full), last_low, CONTRACT_LAST, preferred_element_type=fl_type
    ) + lax.dot_general(first_grad, first_low, CONTRACT_LAST, preferred_element_type=fl_type)
    branch_partial = jnp.dot(
        after(hidden, normed_two_partial), contract_low, preferred_element_type=fl_type
    )
    normed_two_grad = scatter_tokens(normed_two_partial, lambda: (branch_partial,))
    middle_pull = jax.vjp(normalize, middle, gain_rows[1])[1]
    middle_part, gain_two_grad = middle_pull(normed_two_grad)
    middle_grad = out_grad + middle_part
    attended_all = gather_tokens(middle_grad.astype(bf_type))
    contract_sent = owned_sent(after(contract_reduced, middle_grad))
    mixing_full = lax.dot_general(
        mixed, attended_all, CONTRACT_FIRST, preferred_element_type=fl_type
    ).astype(bf_type)
    mixing_reduced = reduce_owned(mixing_full)
    attended_all = after(attended_all, mixing_full)
    mixed_grad = (
        lax.dot_general(attended_all, mixing_low, CONTRACT_LAST, preferred_element_type=fl_type)
        .astype(bf_type)
        .reshape(token_count, head_count, HEAD_DIM)
    )
    mixed_grad = after(mixed_grad, last_reduced)
    last_parts = spread(last_reduced)
    query_grads = []
    key_grads = []
    value_grads = []
    for group_index in range(2):
        if group_index == 1:
            mixed_grad = after(mixed_grad, query_grads[0])
        for kv_index in range(kv_count):
            query_block, key_block, masked = head_scores(group_index, kv_index)
            soft_exact = jnp.exp(masked - log_totals[group_index, kv_index])
            out_block = part(mixed_grad, group_index, kv_index, group_ratio)
            prob_grad = jnp.einsum(
                "gre,ke->rgk",
                out_block,
                part(values, group_index, kv_index, 1)[:, 0],
                preferred_element_type=fl_type,
            )
            inner_sum = jnp.sum(prob_grad * soft_exact, axis=-1, keepdims=True)
            score_grad = (soft_exact * (prob_grad - inner_sum)).astype(bf_type)
            query_grads.append(
                jnp.einsum("rgk,ke->gre", score_grad, key_block, preferred_element_type=fl_type)
                * factor
            )
            key_grads.append(
                jnp.einsum("rgk,gre->ke", score_grad, query_block, preferred_element_type=fl_type)
                * factor
            )
            value_grads.append(
                jnp.einsum(
                    "rgk,gre->ke",
                    soft_exact.astype(bf_type),
                    out_block,
                    preferred_element_type=fl_type,
                )
            )

    def assemble(blocks, axis):
        return jnp.concatenate(
            [
                jnp.concatenate(blocks[:kv_count], axis=axis),
                jnp.concatenate(blocks[kv_count:], axis=axis),
            ]
        )

    query_back = (
        rotate(assemble(query_grads, 1), cosine_table, -sine_table)
        .astype(bf_type)
        .reshape(token_count, query_width)
    )
    key_back = rotate(
        assemble(key_grads, 1).reshape(token_count, kv_count, HEAD_DIM), cosine_table, -sine_table
    ).reshape(token_count, key_width)
    value_back = assemble(value_grads, 1)
    qkv_back = jnp.concatenate(
        [query_back, key_back.astype(bf_type), value_back.astype(bf_type)], axis=1
    )
    expand_states = [expand_weight, expand_moment, expand_second, expand_shadow]
    branch = scatter_tokens(
        branch_partial, lambda: (query_grads[-1],), hold=(attended_all,)
    )
    layer_output = (middle + branch).astype(bf_type)
    contract_news = adamw(
        owned_total(*contract_sent),
        contract_weight,
        contract_moment,
        contract_second,
        contract_shadow,
        MATRIX_RATE,
        WEIGHT_DECAY,
        EMA_KEEP,
    )
    qkv_back = after(qkv_back, layer_output, *contract_sent)
    qkv_full = lax.dot_general(
        normed_all, qkv_back, CONTRACT_FIRST, preferred_element_type=fl_type
    ).astype(bf_type)
    qkv_blocks = low_blocks(qkv_full, 4)
    qkv_moved = sent_low(qkv_blocks)
    normed_partial = lax.dot_general(
        after(qkv_back, last_parts, *qkv_blocks), qkv_low, CONTRACT_LAST, preferred_element_type=fl_type
    )
    first_parts = spread(after(first_reduced, normed_partial))
    normed_kept, normed_sent = token_sums(normed_partial)
    normed_away = swap_pair(normed_sent)
    qkv_total = total_low(after(qkv_moved, normed_sent))
    normed_away = after(normed_away, first_parts, qkv_total, *contract_news)
    normed_grad = normed_kept + normed_away.astype(fl_type)
    expand_news = expand_update((first_parts, last_parts), expand_states)
    qkv_parts = after(columns_moved(qkv_total), *expand_news)
    mixing_grad = owned_total(*owned_sent(after(mixing_reduced, first_parts)))
    rows_pull = jax.vjp(normalize, input_rows, gain_rows[0])[1]
    rows_part, gain_one_grad = rows_pull(normed_grad)
    input_grad = middle_grad + rows_part
    gain_parts = after(jnp.stack([gain_one_grad, gain_two_grad]), first_parts).reshape(2, 2 * dp_count, -1)
    gain_sums = jnp.sum(
        lax.all_to_all(gain_parts, ("dp", "tensor"), split_axis=1, concat_axis=1, tiled=True),
        axis=1,
    )
    (
        (query_master, query_momentum, query_variance, query_average),
        (keyval_master, keyval_momentum, keyval_variance, keyval_average),
    ) = projection_update(
        qkv_parts,
        pair_bit,
        [query_weight, query_moment, query_second, query_shadow],
        [keyval_weight, keyval_moment, keyval_second, keyval_shadow],
    )
    mixing_master, mixing_momentum, mixing_variance, mixing_average = adamw(
        mixing_grad,
        mixing_weight,
        mixing_moment,
        mixing_second,
        mixing_shadow,
        MATRIX_RATE,
        WEIGHT_DECAY,
        EMA_KEEP,
    )
    expand_master, expand_momentum, expand_variance, expand_average = expand_news
    contract_master, contract_momentum, contract_variance, contract_average = contract_news
    norms_master, norms_momentum, norms_variance, norms_average = adamw(
        gain_sums, norms_weight, norms_moment, norms_second, norms_shadow, GAIN_RATE, 0.0, GAIN_KEEP
    )
    return (
        layer_output,
        input_grad,
        query_master,
        query_momentum,
        query_variance,
        query_average,
        keyval_master,
        keyval_momentum,
        keyval_variance,
        keyval_average,
        mixing_master,
        mixing_momentum,
        mixing_variance,
        mixing_average,
        expand_master,
        expand_momentum,
        expand_variance,
        expand_average,
        contract_master,
        contract_momentum,
        contract_variance,
        contract_average,
        norms_master,
        norms_momentum,
        norms_variance,
        norms_average,
    )


def solution(mesh):
    in_specs = (
        P(("dp", "tensor"), None),
        P(("dp", "tensor"), None),
        P("dp", None),
        P("dp", None),
        P("dp", "tensor"),
        P("dp", "tensor"),
        P("dp", "tensor"),
        P("dp", "tensor"),
        P("dp", None, "tensor"),
        P("dp", None, "tensor"),
        P("dp", None, "tensor"),
        P("dp", None, "tensor"),
        P(("tensor", "dp"), None),
        P(("tensor", "dp"), None),
        P(("tensor", "dp"), None),
        P(("tensor", "dp"), None),
        P("dp", None, "tensor"),
        P("dp", None, "tensor"),
        P("dp", None, "tensor"),
        P("dp", None, "tensor"),
        P(("tensor", "dp"), None),
        P(("tensor", "dp"), None),
        P(("tensor", "dp"), None),
        P(("tensor", "dp"), None),
        P(None, ("dp", "tensor")),
        P(None, ("dp", "tensor")),
        P(None, ("dp", "tensor")),
        P(None, ("dp", "tensor")),
    )
    out_specs = (
        P(("dp", "tensor"), None),
        P(("dp", "tensor"), None),
        P("dp", "tensor"),
        P("dp", "tensor"),
        P("dp", "tensor"),
        P("dp", "tensor"),
        P("dp", None, "tensor"),
        P("dp", None, "tensor"),
        P("dp", None, "tensor"),
        P("dp", None, "tensor"),
        P(("tensor", "dp"), None),
        P(("tensor", "dp"), None),
        P(("tensor", "dp"), None),
        P(("tensor", "dp"), None),
        P("dp", None, "tensor"),
        P("dp", None, "tensor"),
        P("dp", None, "tensor"),
        P("dp", None, "tensor"),
        P(("tensor", "dp"), None),
        P(("tensor", "dp"), None),
        P(("tensor", "dp"), None),
        P(("tensor", "dp"), None),
        P(None, ("dp", "tensor")),
        P(None, ("dp", "tensor")),
        P(None, ("dp", "tensor")),
        P(None, ("dp", "tensor")),
    )
    return jax.shard_map(
        per_device, mesh=mesh, in_specs=in_specs, out_specs=out_specs, check_vma=False
    )
```
